32 devices in a mesh: seq: 4 (over z), shard: 8 (over y, x, core).
Axes of the slice: x: 2, y: 2, z: 4, core: 2. Of those that a mesh axis runs over, the one named last changes fastest.
Arguments:
- tokens_in: bfloat16 [8, 512, 1024], P('shard', 'seq'), may hold values from -6 to 6
- out_grad: bfloat16 [8, 512, 1024], P('shard', 'seq'), may hold values from -6 to 6
- segments: int32 [8, 512], P('shard'), may hold values from 0 to 3, never falling along the last dimension, each value on 1 to 256 neighbouring positions
- w_qkv: float32 [1024, 3072], P(('seq', 'shard'))
- w_out: float32 [1024, 1024], P(('seq', 'shard')), may hold values from -0.375 to 0.375
- w_up: float32 [1024, 4096], P(('seq', 'shard')), may hold values from -0.1875 to 0.1875
- w_down: float32 [1024, 4096], P(('seq', 'shard')), may hold values from -0.09375 to 0.09375
- vectors: float32 [12288], P(('seq', 'shard'))
- mom_qkv: float32 [1024, 3072], P(('seq', 'shard')), may hold values from -56 to 56
- mom_out: float32 [1024, 1024], P(('seq', 'shard')), may hold values from -56 to 56
- mom_up: float32 [1024, 4096], P(('seq', 'shard')), may hold values from -40 to 40
- mom_down: float32 [1024, 4096], P(('seq', 'shard')), may hold values from -56 to 56
- mom_vectors: float32 [12288], P(('seq', 'shard')), may hold values from -80 to 80
Outputs:
- block_out: bfloat16 [8, 512, 1024], P('shard', 'seq')
- grad_inputs: float32 [8, 512, 1024], P('shard', 'seq')
- grad_qkv: float32 [1024, 3072], P(('seq', 'shard'))
- grad_out: float32 [1024, 1024], P(('seq', 'shard'))
- grad_up: float32 [1024, 4096], P(('seq', 'shard'))
- grad_down: float32 [1024, 4096], P(('seq', 'shard'))
- grad_vectors: float32 [12288], P(('seq', 'shard'))
- new_qkv: float32 [1024, 3072], P(('seq', 'shard'))
- new_out: float32 [1024, 1024], P(('seq', 'shard'))
- new_up: float32 [1024, 4096], P(('seq', 'shard'))
- new_down: float32 [1024, 4096], P(('seq', 'shard'))
- new_vectors: float32 [12288], P(('seq', 'shard'))
- next_mom_qkv: float32 [1024, 3072], P(('seq', 'shard'))
- next_mom_out: float32 [1024, 1024], P(('seq', 'shard'))
- next_mom_up: float32 [1024, 4096], P(('seq', 'shard'))
- next_mom_down: float32 [1024, 4096], P(('seq', 'shard'))
- next_mom_vectors: float32 [12288], P(('seq', 'shard'))
The draws below stay inside these ranges and needn't reach their ends.
Inputs may be any that keep to these rules, and one draw needn't show every extreme that they name: `segments`: each row's document ids never fall; a document holds at most 256 positions.
All inputs are finite; a program needn't handle non-finite values.
Results may differ from the reference program's by a relative error of at most 0.012.
Values may be sent and summed in bfloat16 or wider, within the bound.
No kernel may reach another device: no remote copies, remote signals or barrier semaphores. Data moves between devices by JAX's collectives and lax.ppermute only.
A program may use at most 192 MiB of HBM per device.

```python
import math
import jax
import jax.numpy as jnp
import numpy as np
from jax import lax

D = 1024
H = 16
HD = 64
FF = 4096
NS_ITERS = 3
DOCS = 4
SEQ = 512
SEQS = 8
TOKENS = 4096
DOC_MOST = 256
VEC = 12288


def draw_w_qkv(key, part):
    base = jax.random.normal(key, (D, 3 * D), jnp.float32) * D ** (-0.5)
    return base


def draw_vectors(key, part):
    first_key, second_key = jax.random.split(key)
    row_of = jnp.arange(12 * D) // D
    is_gain = (row_of == 0) | (row_of == 5)
    gains = jax.random.uniform(first_key, (12 * D,), jnp.float32, 0.5, 1.5)
    biases = jax.random.normal(second_key, (12 * D,), jnp.float32) * 0.3
    return jnp.where(is_gain, gains, biases)


def levels(stream_key, shape, shards, least, high):
    def one(axis_at, shards_of):
        draws = jax.random.uniform(jax.random.fold_in(jax.random.fold_in(stream_key, 6), axis_at), (shards_of,), jnp.float32, least / len(shards), high / len(shards))
        return jnp.repeat(jnp.exp(draws), shape[axis_at] // shards_of).reshape((-1,) + (1,) * (len(shape) - axis_at - 1))

    factor_of = one(*shards[0])
    for cut in shards[1:]:
        factor_of = factor_of * one(*cut)
    return factor_of


def profile(amount, total, limit, lean):
    weights = [(1 << 20) // math.isqrt(standing ** lean) + 1 for standing in range(2, amount + 1)]
    rest, given = total - limit - (amount - 1), [1] * (amount - 1)
    while rest > 0:
        candidates = [i for i in range(amount - 1) if given[i] < limit]
        mass, budget = sum([weights[i] for i in candidates]), rest
        for i in candidates:
            more = min(limit - given[i], max(1, budget * weights[i] // mass), rest)
            given[i] = given[i] + more
            rest = rest - more
    return np.array([limit] + given)


def uneven(rng, number_of, total, limit, skew):
    if number_of == 2:
        one = jax.random.randint(rng, (), max(1, total - limit), min(limit, total - 1) + 1)
        return jnp.stack([one, total - one])
    tallies = jnp.asarray(profile(number_of, total, limit, skew), jnp.int32)
    pairs = (number_of - 1) // 2
    giver, taker = tallies[1:1 + 2 * pairs:2], tallies[2:2 + 2 * pairs:2]
    margin = jnp.minimum(giver - 1, limit - taker)
    moved = jax.random.randint(jax.random.fold_in(rng, 1), (pairs,), 0, 1 << 20) % (margin + 1)
    tallies = tallies.at[1:1 + 2 * pairs:2].set(giver - moved).at[2:2 + 2 * pairs:2].set(taker + moved)
    return tallies[jax.random.permutation(jax.random.fold_in(rng, 2), number_of)]


def centred(own_key, extent, width, limit, cuts=(), held_as=jnp.bfloat16):
    entries = jax.random.normal(own_key, extent, jnp.float32) * width
    if len(cuts) > 0:
        entries = levels(own_key, extent, cuts, -0.22, 0.18) * entries
    return jnp.clip(entries, min=-limit, max=limit).astype(held_as)


def setup_inputs(seed: int = 0) -> dict:
    splits = jax.random.split(jax.random.key(seed), 14)
    tokens_in = centred(splits[0], (SEQS, SEQ, D), 1.0, 6.0, ((0, 8), (1, 4)))
    out_grad = centred(splits[1], (SEQS, SEQ, D), 1.0, 6.0, ((0, 8), (1, 4)))
    segments = jax.vmap(lambda own: jnp.searchsorted(jnp.cumsum(uneven(own, DOCS, SEQ, DOC_MOST, 0)), jnp.arange(SEQ), side="right"))(jax.random.split(splits[2], SEQS)).reshape((SEQS, SEQ)).astype(jnp.int32)
    w_qkv = draw_w_qkv(jax.random.fold_in(splits[13], 71), 0)
    w_out = centred(splits[4], (D, D), (D // 4) ** -0.5, 0.375, ((0, 32),), jnp.float32)
    w_up = centred(splits[5], (D, FF), D ** -0.5, 0.1875, ((0, 32),), jnp.float32)
    w_down = centred(splits[6], (D, FF), FF ** -0.5, 0.09375, ((0, 32),), jnp.float32)
    vectors = draw_vectors(jax.random.fold_in(splits[13], 71), 0)
    mom_qkv = centred(splits[8], (D, 3 * D), (0.15 * TOKENS ** 0.5), 56.0, ((0, 32),), jnp.float32)
    mom_out = centred(splits[9], (D, D), (0.15 * TOKENS ** 0.5), 56.0, ((0, 32),), jnp.float32)
    mom_up = centred(splits[10], (D, FF), (0.1 * TOKENS ** 0.5), 40.0, ((0, 32),), jnp.float32)
    mom_down = centred(splits[11], (D, FF), (0.15 * TOKENS ** 0.5), 56.0, ((0, 32),), jnp.float32)
    mom_vectors = centred(splits[12], (VEC,), (0.2 * TOKENS ** 0.5), 80.0, ((0, 32),), jnp.float32)
    return {"tokens_in": tokens_in, "out_grad": out_grad, "segments": segments, "w_qkv": w_qkv, "w_out": w_out, "w_up": w_up, "w_down": w_down, "vectors": vectors, "mom_qkv": mom_qkv, "mom_out": mom_out, "mom_up": mom_up, "mom_down": mom_down, "mom_vectors": mom_vectors}


newton_coefs = (3.4445, -4.775, 2.0315)
momentum_decay = 0.9
matrix_rate = 0.1
vector_rate = 0.2
highest = lax.Precision.HIGHEST

def layer_norm(values, gain_vec, shift_vec):
    center = values - lax.optimization_barrier(jnp.mean(values, axis=-1, keepdims=True))
    spread = lax.optimization_barrier(jnp.mean(center * center, axis=-1, keepdims=True))
    return center * lax.rsqrt(spread + 1e-05) * gain_vec + shift_vec

def gelu_tanh(values):
    return jax.nn.gelu(values, approximate=True)

def unpack(flat_vec):
    rows = flat_vec.reshape(12, D)
    return (rows[0], rows[1], rows[2], rows[3], rows[4], rows[5], rows[6], rows[7:11].reshape(FF), rows[11])

def head_slopes(first_head, head_count):
    heads = (first_head + jnp.arange(head_count)).astype(jnp.float32)
    return jnp.exp2(-8.0 * (heads + 1.0) / H)

def all_scores(query, key_rows, seg_row, slopes):
    scores = jnp.einsum('qhd,khd->hqk', query.astype(jnp.float32), key_rows.astype(jnp.float32)) * HD ** (-0.5)
    positions = jnp.arange(SEQ)
    distance = (positions[:, None] - positions[None, :]).astype(jnp.float32)
    scores = scores - slopes[:, None, None] * distance[None]
    allowed = (distance >= 0) & (seg_row[:, None] == seg_row[None, :])
    return jnp.where(allowed[None], scores, -1e+30)

def one_sequence(tokens_seq, cotangent, seg_row, matrices, params):
    full_qkv, full_out, full_up, full_down = matrices
    gain_one, shift_one, bias_query, bias_value, bias_out, gain_two, shift_two, bias_up, bias_down = params
    residual = tokens_seq.astype(jnp.float32)
    hidden_one = layer_norm(residual, gain_one, shift_one).astype(jnp.bfloat16)
    qkv_bias = jnp.concatenate([bias_query, jnp.zeros((D,), jnp.float32), bias_value])
    qkv_mixed = jnp.dot(hidden_one, full_qkv, preferred_element_type=jnp.float32) + qkv_bias
    query = qkv_mixed[:, :D].astype(jnp.bfloat16).reshape(SEQ, H, HD)
    key_rows = qkv_mixed[:, D:2 * D].astype(jnp.bfloat16).reshape(SEQ, H, HD)
    value_rows = qkv_mixed[:, 2 * D:].astype(jnp.bfloat16).reshape(SEQ, H, HD)
    slopes = head_slopes(0, H)
    scores = all_scores(query, key_rows, seg_row, slopes)
    row_max = lax.optimization_barrier(jnp.max(scores, axis=-1, keepdims=True))
    exp_terms = jnp.exp(scores - row_max)
    row_total = lax.optimization_barrier(jnp.sum(exp_terms, axis=-1, keepdims=True))
    logsum = row_max + jnp.log(row_total)
    prob_rows = (exp_terms / row_total).astype(jnp.bfloat16)
    attended = jnp.einsum('hqk,khd->qhd', prob_rows.astype(jnp.float32), value_rows.astype(jnp.float32))
    attended = attended.astype(jnp.bfloat16).reshape(SEQ, D)
    middle = residual + jnp.dot(attended, full_out, preferred_element_type=jnp.float32) + bias_out
    hidden_two = layer_norm(middle, gain_two, shift_two).astype(jnp.bfloat16)
    before = jnp.dot(hidden_two, full_up, preferred_element_type=jnp.float32) + bias_up
    active = gelu_tanh(before).astype(jnp.bfloat16)
    block_rows = (middle + jnp.dot(active, full_down.T, preferred_element_type=jnp.float32) + bias_down).astype(jnp.bfloat16)
    upstream = cotangent.astype(jnp.float32)
    grad_down = jnp.dot(cotangent.T, active, preferred_element_type=jnp.float32)
    grad_active = jnp.dot(cotangent, full_down, preferred_element_type=jnp.float32)
    grad_before = jax.vjp(gelu_tanh, before)[1](grad_active)[0]
    grad_before_b = grad_before.astype(jnp.bfloat16)
    grad_up = jnp.dot(hidden_two.T, grad_before_b, preferred_element_type=jnp.float32)
    grad_hidden_two = jnp.dot(grad_before_b, full_up.T, preferred_element_type=jnp.float32)
    middle_part, grad_gain_two, grad_shift_two = jax.vjp(layer_norm, middle, gain_two, shift_two)[1](grad_hidden_two)
    grad_middle = upstream + middle_part
    grad_middle_b = grad_middle.astype(jnp.bfloat16)
    grad_out = jnp.dot(attended.T, grad_middle_b, preferred_element_type=jnp.float32)
    grad_attended = jnp.dot(grad_middle_b, full_out.T, preferred_element_type=jnp.float32).astype(jnp.bfloat16).reshape(SEQ, H, HD)
    prob_again = jnp.exp(scores - logsum)
    prob_again_b = prob_again.astype(jnp.bfloat16)
    grad_values = jnp.einsum('hqk,qhd->khd', prob_again_b.astype(jnp.float32), grad_attended.astype(jnp.float32))
    grad_probs = jnp.einsum('qhd,khd->hqk', grad_attended.astype(jnp.float32), value_rows.astype(jnp.float32))
    row_inner = lax.optimization_barrier(jnp.sum(prob_again * grad_probs, axis=-1, keepdims=True))
    grad_scores = (prob_again * (grad_probs - row_inner) * HD ** (-0.5)).astype(jnp.bfloat16)
    grad_query = jnp.einsum('hqk,khd->qhd', grad_scores.astype(jnp.float32), key_rows.astype(jnp.float32))
    grad_keys = jnp.einsum('hqk,qhd->khd', grad_scores.astype(jnp.float32), query.astype(jnp.float32))
    grad_query_b = grad_query.astype(jnp.bfloat16).reshape(SEQ, D)
    grad_keys_b = grad_keys.astype(jnp.bfloat16).reshape(SEQ, D)
    grad_values_b = grad_values.astype(jnp.bfloat16).reshape(SEQ, D)
    grad_mixed = jnp.concatenate([grad_query_b, grad_keys_b, grad_values_b], axis=1)
    grad_qkv = jnp.dot(hidden_one.T, grad_mixed, preferred_element_type=jnp.float32)
    grad_hidden_one = jnp.dot(grad_mixed, full_qkv.T, preferred_element_type=jnp.float32)
    input_part, grad_gain_one, grad_shift_one = jax.vjp(layer_norm, residual, gain_one, shift_one)[1](grad_hidden_one)
    grad_rows = grad_middle + input_part
    grad_vec = jnp.concatenate([grad_gain_one, grad_shift_one, lax.optimization_barrier(jnp.sum(grad_query_b.astype(jnp.float32), axis=0)), lax.optimization_barrier(jnp.sum(grad_values_b.astype(jnp.float32), axis=0)), lax.optimization_barrier(jnp.sum(grad_middle, axis=0)), grad_gain_two, grad_shift_two, lax.optimization_barrier(jnp.sum(grad_before, axis=0)), lax.optimization_barrier(jnp.sum(upstream, axis=0))])
    return (block_rows, grad_rows, (grad_qkv, grad_out, grad_up, grad_down, grad_vec))

def orthogonalize(matrix):
    current = matrix / (jnp.sqrt(jnp.sum(matrix * matrix)) + 1e-07)
    for sweep_index in range(NS_ITERS):
        gram_matrix = jnp.dot(current, current.T, precision=highest)
        one_product = jnp.dot(gram_matrix, current, precision=highest)
        two_product = jnp.dot(gram_matrix, one_product, precision=highest)
        current = newton_coefs[0] * current + newton_coefs[1] * one_product + newton_coefs[2] * two_product
    return current

def reference(tokens_in, out_grad, segments, w_qkv, w_out, w_up, w_down, vectors, mom_qkv, mom_out, mom_up, mom_down, mom_vectors):
    matrices = (w_qkv.astype(jnp.bfloat16), w_out.astype(jnp.bfloat16), w_up.astype(jnp.bfloat16), w_down.astype(jnp.bfloat16))
    params = unpack(lax.optimization_barrier(vectors.astype(jnp.bfloat16)).astype(jnp.float32))

    def scan_step(carry, inputs):
        tokens_seq, cotangent, seg_row = inputs
        block_rows, grad_rows, grads = one_sequence(tokens_seq, cotangent, seg_row, matrices, params)
        carry = jax.tree.map(lambda total_part, new_part: total_part + new_part, carry, grads)
        return (carry, (block_rows, grad_rows))
    start_carry = (jnp.zeros((D, 3 * D), jnp.float32), jnp.zeros((D, D), jnp.float32), jnp.zeros((D, FF), jnp.float32), jnp.zeros((D, FF), jnp.float32), jnp.zeros((VEC,), jnp.float32))
    grads, stacked = lax.scan(scan_step, start_carry, (tokens_in, out_grad, segments))
    block_out, grad_inputs = stacked
    grad_qkv, grad_out, grad_up, grad_down, grad_vec = grads

    def muon(weight, moment, gradient):
        next_moment = momentum_decay * moment + gradient
        ortho = orthogonalize(next_moment)
        return (weight - matrix_rate * 0.2 * math.sqrt(weight.shape[1]) * ortho, next_moment)
    new_qkv, next_mom_qkv = muon(w_qkv, mom_qkv, grad_qkv)
    new_out, next_mom_out = muon(w_out, mom_out, grad_out)
    new_up, next_mom_up = muon(w_up, mom_up, grad_up)
    new_down, next_mom_down = muon(w_down, mom_down, grad_down)
    next_mom_vectors = momentum_decay * mom_vectors + grad_vec
    new_vectors = vectors - vector_rate / math.sqrt(TOKENS) * next_mom_vectors
    return (block_out, grad_inputs, grad_qkv, grad_out, grad_up, grad_down, grad_vec, new_qkv, new_out, new_up, new_down, new_vectors, next_mom_qkv, next_mom_out, next_mom_up, next_mom_down, next_mom_vectors)
```

```python
import functools
import math

import jax
import jax.numpy as jnp
from jax import lax
from jax.experimental import pallas as pl
from jax.experimental.pallas import tpu as pltpu
from jax.sharding import PartitionSpec as P

D = 1024
H = 16
HD = 64
FF = 4096
VEC = 12 * D

ca, cb, cc = (3.4445, -4.775, 2.0315)
momentum_decay = 0.9
matrix_rate = 0.1
vector_rate = 0.2
f32 = jnp.float32
b16 = jnp.bfloat16


def layer_norm(values, gain_vec, shift_vec):
    center = values - jnp.mean(values, axis=-1, keepdims=True)
    spread = jnp.mean(center * center, axis=-1, keepdims=True)
    return center * lax.rsqrt(spread + 1e-05) * gain_vec + shift_vec


def normed(values):
    center = values - jnp.mean(values, axis=-1, keepdims=True)
    spread = jnp.mean(center * center, axis=-1, keepdims=True)
    return center * lax.rsqrt(spread + 1e-05)


def gelu_tanh(values):
    return jax.nn.gelu(values, approximate=True)


def dot(a, b):
    return jnp.dot(a, b, preferred_element_type=f32)


def dot_nt(a, b):
    return lax.dot_general(a, b, (((1,), (1,)), ((), ())), preferred_element_type=f32)


def dot_tn(a, b):
    return lax.dot_general(a, b, (((0,), (0,)), ((), ())), preferred_element_type=f32)


def spans(total):
    rows = 128
    reach = total // 2
    out = []
    for begin in range(0, total, rows):
        first = max(0, begin - reach + 1) // 128 * 128
        out.append((begin, rows, first, begin + rows - first))
    return out


def probabilities(q, k, seg_q, seg_k, slope, offset):
    scores = dot_nt(q, k) * HD ** (-0.5)
    shape = scores.shape
    distance = offset + lax.broadcasted_iota(jnp.int32, shape, 0) - lax.broadcasted_iota(
        jnp.int32, shape, 1
    )
    scores = scores - slope * distance.astype(f32)
    scores = jnp.where((distance >= 0) & (seg_q == seg_k), scores, -1e30)
    terms = jnp.exp(scores - jnp.max(scores, axis=-1, keepdims=True))
    return terms * (1.0 / jnp.sum(terms, axis=-1, keepdims=True))


def attend_kernel(slopes, seg_col, seg_row, q, k, v, out):
    pair = pl.program_id(0)
    for j in range(2):
        cols = slice(j * HD, (j + 1) * HD)
        slope = slopes[2 * pair + j]
        for begin, rows, first, wide in spans(q.shape[0]):
            keys = slice(first, first + wide)
            probs = probabilities(
                q[begin : begin + rows, cols],
                k[keys, cols],
                seg_col[begin : begin + rows, :],
                seg_row[:, keys],
                slope,
                begin - first,
            )
            out[begin : begin + rows, cols] = dot(probs.astype(b16), v[keys, cols]).astype(b16)


def attend_back_kernel(slopes, seg_col, seg_row, q, k, v, g, dq, dk, dv, k_acc, v_acc):
    pair = pl.program_id(0)
    k_acc[...] = jnp.zeros_like(k_acc)
    v_acc[...] = jnp.zeros_like(v_acc)
    for j in range(2):
        cols = slice(j * HD, (j + 1) * HD)
        slope = slopes[2 * pair + j]
        for begin, rows, first, wide in spans(q.shape[0]):
            keys = slice(first, first + wide)
            q_block = q[begin : begin + rows, cols]
            g_block = g[begin : begin + rows, cols]
            probs = probabilities(
                q_block,
                k[keys, cols],
                seg_col[begin : begin + rows, :],
                seg_row[:, keys],
                slope,
                begin - first,
            )
            v_acc[keys, cols] += dot_tn(probs.astype(b16), g_block)
            grad_probs = dot_nt(g_block, v[keys, cols])
            inner = jnp.sum(probs * grad_probs, axis=-1, keepdims=True)
            grad_scores = (probs * (grad_probs - inner) * HD ** (-0.5)).astype(b16)
            dq[begin : begin + rows, cols] = dot(grad_scores, k[keys, cols]).astype(b16)
            k_acc[keys, cols] += dot_tn(grad_scores, q_block)
    dk[...] = k_acc[...].astype(b16)
    dv[...] = v_acc[...].astype(b16)


def attention_specs(total, pairs):
    col = pl.BlockSpec((total, 1), lambda p: (0, 0))
    row = pl.BlockSpec((1, total), lambda p: (0, 0))
    parts = [
        pl.BlockSpec((total, 2 * HD), lambda p, base=base: (0, base * pairs + p))
        for base in range(3)
    ]
    return [pl.BlockSpec(memory_space=pltpu.SMEM), col, row] + parts


def attend(slopes, seg, qkv):
    total = qkv.shape[0]
    wide = qkv.shape[1] // 3
    pairs = wide // (2 * HD)
    return pl.pallas_call(
        attend_kernel,
        grid=(pairs,),
        out_shape=jax.ShapeDtypeStruct((total, wide), b16),
        in_specs=attention_specs(total, pairs),
        out_specs=pl.BlockSpec((total, 2 * HD), lambda p: (0, p)),
        compiler_params=pltpu.CompilerParams(vmem_limit_bytes=24 * 2**20),
    )(slopes, seg.reshape(total, 1), seg.reshape(1, total), qkv, qkv, qkv)


def attend_back(slopes, seg, qkv, grad):
    total = qkv.shape[0]
    wide = qkv.shape[1] // 3
    pairs = wide // (2 * HD)
    pair_spec = pl.BlockSpec((total, 2 * HD), lambda p: (0, p))
    part = jax.ShapeDtypeStruct((total, wide), b16)
    return pl.pallas_call(
        attend_back_kernel,
        grid=(pairs,),
        out_shape=(part, part, part),
        in_specs=attention_specs(total, pairs) + [pair_spec],
        out_specs=(pair_spec, pair_spec, pair_spec),
        scratch_shapes=[pltpu.VMEM((total, 2 * HD), f32), pltpu.VMEM((total, 2 * HD), f32)],
        compiler_params=pltpu.CompilerParams(vmem_limit_bytes=24 * 2**20),
    )(slopes, seg.reshape(total, 1), seg.reshape(1, total), qkv, qkv, qkv, grad)


def shift_seq(array, groups, k):
    return lax.ppermute(array, "seq", [(i, (i + k) % groups) for i in range(groups)])


def flip_shard(array, shards, bit):
    return lax.ppermute(array, "shard", [(i, i ^ (1 << bit)) for i in range(shards)])


def gather_seq(array, groups, z, axis):
    size = array.shape[axis]
    shape = list(array.shape)
    shape[axis] = size * groups
    full = jnp.zeros(shape, array.dtype)
    full = lax.dynamic_update_slice_in_dim(full, array, z * size, axis)
    for k in range(1, groups):
        piece = shift_seq(array, groups, k)
        full = lax.dynamic_update_slice_in_dim(full, piece, (z - k) % groups * size, axis)
    return full


def reduce_seq(array, groups, z):
    size = array.shape[0] // groups
    total = lax.dynamic_slice_in_dim(array, z * size, size, 0)
    for k in range(1, groups):
        block = lax.dynamic_slice_in_dim(array, (z + k) % groups * size, size, 0)
        total = total + shift_seq(block.astype(b16), groups, k).astype(f32)
    return total


def gather_seq_line(array, groups, z):
    right, left = [array], [array]
    for _ in range(groups - 1):
        right.append(lax.ppermute(right[-1], "seq", [(i, i + 1) for i in range(groups - 1)]))
        left.append(lax.ppermute(left[-1], "seq", [(i + 1, i) for i in range(groups - 1)]))
    pieces = [array]
    for k in range(1, groups):
        pieces.append(jnp.where(z >= k, right[k], left[groups - k]))
    return pieces


def halve(array, shards, s, bits, order, keep_first=None):
    left = list(bits)
    out = array
    for b in order:
        ax = left.index(b)
        mine = (s >> b) & 1
        keep = lax.dynamic_index_in_dim(out, mine, ax, False)
        give = lax.dynamic_index_in_dim(out, 1 - mine, ax, False)
        got = flip_shard(give, shards, b)
        left.pop(ax)
        out = keep.astype(f32) + got.astype(f32)
        if left:
            out = out.astype(b16)
    return out


def pad_to(array, wide):
    return jnp.pad(array, ((0, 0), (0, wide - array.shape[1])))


def per_device(
    tokens_in,
    out_grad,
    segments,
    w_qkv,
    w_out,
    w_up,
    w_down,
    vectors,
    mom_qkv,
    mom_out,
    mom_up,
    mom_down,
    mom_vectors,
):
    groups = lax.axis_size("seq")
    shards = lax.axis_size("shard")
    z = lax.axis_index("seq")
    s = lax.axis_index("shard")
    length = tokens_in.shape[1]
    total = length * groups
    rows = w_qkv.shape[0]
    owners = shards // 4
    part_d = D // groups
    part_f = FF // groups
    wide = part_f // owners
    chunk = vectors.shape[0]

    def columns_of(matrix, parts):
        split = matrix.astype(b16).reshape(rows, parts, groups, -1)
        return split.transpose(2, 0, 1, 3).reshape(groups, rows, -1)

    lanes = min(chunk, 128)
    vec_rows = chunk // lanes
    vec_block = jnp.pad(
        vectors.astype(b16).reshape(vec_rows, lanes), ((0, rows - vec_rows), (0, 128 - lanes))
    )
    send_a = jnp.concatenate(
        [columns_of(w_qkv, 3), jnp.broadcast_to(vec_block, (groups, rows, 128))], axis=2
    )
    got_a = lax.all_to_all(send_a, "seq", 0, 0)
    send_b = jnp.concatenate(
        [
            jnp.broadcast_to(w_out.astype(b16), (groups, rows, D)),
            columns_of(w_up, 1),
            columns_of(w_down, 1),
        ],
        axis=2,
    )
    residual = gather_seq(tokens_in[0], groups, z, 0).astype(f32)
    all_a = lax.all_gather(got_a, "shard", axis=1).reshape(groups * shards, rows, -1)
    part_qkv = all_a[:, :, : 3 * part_d].reshape(D, 3 * part_d)
    full_vec = all_a[:, :vec_rows, 3 * part_d : 3 * part_d + lanes].reshape(VEC).astype(f32).reshape(12, D)
    send_b, got_a = lax.optimization_barrier((send_b, got_a))
    got_b = lax.all_to_all(send_b, "seq", 0, 0)
    all_b = lax.all_gather(got_b, "shard", axis=1).reshape(D, -1)
    full_out = all_b[:, :D]
    part_up = all_b[:, D : D + part_f]
    part_down = all_b[:, D + part_f :]

    gain_one, shift_one, bias_query, bias_value, bias_out, gain_two, shift_two = (
        full_vec[i] for i in range(7)
    )
    bias_up = lax.dynamic_slice_in_dim(full_vec[7:11].reshape(FF), z * part_f, part_f, 0)
    bias_down = full_vec[11]
    part_bias = jnp.concatenate(
        [
            lax.dynamic_slice_in_dim(bias_query, z * part_d, part_d, 0),
            jnp.zeros((part_d,), f32),
            lax.dynamic_slice_in_dim(bias_value, z * part_d, part_d, 0),
        ]
    )

    normed_one = normed(residual)
    hidden_one = (normed_one * gain_one + shift_one).astype(b16)
    qkv = (dot(hidden_one, part_qkv) + part_bias).astype(b16)
    head_count = part_d // HD
    heads = (z * head_count + jnp.arange(head_count)).astype(f32)
    slopes = jnp.exp2(-8.0 * (heads + 1.0) / H)
    attended_part = attend(slopes, segments[0], qkv)
    attended = gather_seq(attended_part, groups, z, 1)
    middle = residual + dot(attended, full_out) + bias_out
    normed_two = normed(middle)
    hidden_two = (normed_two * gain_two + shift_two).astype(b16)
    before = dot(hidden_two, part_up) + bias_up
    active = gelu_tanh(before).astype(b16)
    cotangent = gather_seq(out_grad[0], groups, z, 0)
    own_upstream = out_grad[0].astype(f32)

    grad_active = dot(cotangent, part_down)
    grad_before = jax.vjp(gelu_tanh, before)[1](grad_active)[0]
    grad_before_b = grad_before.astype(b16)
    hidden_two_share = dot_nt(grad_before_b, part_up)
    grad_hidden_two = reduce_seq(hidden_two_share, groups, z)
    own_middle = lax.dynamic_slice_in_dim(middle, z * length, length, 0)
    middle_part = jax.vjp(lambda m: layer_norm(m, gain_two, shift_two), own_middle)[1](
        grad_hidden_two
    )[0]
    grad_middle = own_upstream + middle_part
    grad_middle_b = grad_middle.astype(b16)
    grad_attended = dot_nt(grad_middle_b, full_out).astype(b16)

    def to_columns(array):
        blocks = array.reshape(length, groups, part_d).transpose(1, 0, 2)
        return lax.all_to_all(blocks, "seq", 0, 0).reshape(total, part_d)

    head_grad = to_columns(grad_attended)
    middle_cols = to_columns(grad_middle_b)
    grad_q, grad_k, grad_v = attend_back(slopes, segments[0], qkv, head_grad)
    grad_mixed = jnp.concatenate([grad_q, grad_k, grad_v], axis=1)
    hidden_one_share = dot_nt(grad_mixed, part_qkv)

    block_share = dot_nt(active, part_down)
    block_rows = (reduce_seq(block_share, groups, z) + own_middle + bias_down).astype(b16)
    grad_hidden_one = reduce_seq(hidden_one_share, groups, z)
    own_residual = tokens_in[0].astype(f32)
    input_part = jax.vjp(lambda m: layer_norm(m, gain_one, shift_one), own_residual)[1](
        grad_hidden_one
    )[0]
    grad_rows = grad_middle + input_part

    def placed(values, width):
        return lax.dynamic_update_slice_in_dim(jnp.zeros((width,), f32), values, z * values.shape[0], 0)

    share_vec = jnp.concatenate(
        [
            jnp.sum(hidden_one_share * normed_one, axis=0),
            jnp.sum(hidden_one_share, axis=0),
            placed(jnp.sum(grad_q.astype(f32), axis=0), D),
            placed(jnp.sum(grad_v.astype(f32), axis=0), D),
            jnp.sum(grad_middle, axis=0),
            jnp.sum(hidden_two_share * normed_two, axis=0),
            jnp.sum(hidden_two_share, axis=0),
            placed(jnp.sum(grad_before, axis=0), FF),
            jnp.sum(own_upstream, axis=0),
        ]
    )
    vec_area = jnp.pad(
        share_vec.astype(b16).reshape(groups * shards, 1, chunk), ((0, 0), (0, rows - 1), (0, 0))
    ).reshape(D, chunk)

    low = s & 1
    pairs = (
        (hidden_one, grad_mixed),
        (attended, middle_cols),
        (hidden_two, grad_before_b),
        (cotangent, active),
    )

    def half(bit):
        blocks = []
        for index, (left, right) in enumerate(pairs):
            size = right.shape[1] // owners
            for high in range(owners // 2):
                cut = lax.dynamic_slice_in_dim(right, (2 * high + bit) * size, size, 1)
                block = dot_tn(left, cut).astype(b16)
                if index == 1 and high == 0:
                    block = jnp.concatenate(
                        [block, jnp.where(bit == 0, vec_area, jnp.zeros_like(vec_area))], axis=1
                    )
                blocks.append(pad_to(block, wide))
        return jnp.stack(blocks)

    got = flip_shard(half(1 - low), shards, 0)
    summed = (half(low).astype(f32) + got.astype(f32)).astype(b16)
    bit_count = shards.bit_length() - 1
    bits = list(range(bit_count - 1, 0, -1))
    summed = summed.reshape([2] * len(bits) + [D, wide])
    up_order = bits[::-1]
    other_order = up_order[len(bits) // 2 :] + up_order[: len(bits) // 2]
    halves = [
        halve(summed[..., : D // 2, :], shards, s, bits, up_order),
        halve(summed[..., D // 2 :, :], shards, s, bits, other_order),
    ]
    own_grad = jnp.concatenate(halves, axis=0)
    own_grad_b = own_grad.astype(b16)

    def blocks_of(matrix, parts):
        split = matrix.reshape(rows, parts, groups, -1).transpose(0, 2, 1, 3)
        split = split.reshape(rows, groups, owners, -1)
        return jnp.pad(split, ((0, 0), (0, 0), (0, 0), (0, wide - split.shape[3])))

    mom_blocks = jnp.stack(
        [
            blocks_of(mom_qkv.astype(b16), 3),
            blocks_of(mom_out.astype(b16), 1),
            blocks_of(mom_up.astype(b16), 1),
            blocks_of(mom_down.astype(b16), 1),
        ],
        axis=2,
    )
    mom_blocks = mom_blocks.transpose(1, 2, 3, 0, 4).reshape(groups * shards, rows, wide)
    mom_blocks, _ = lax.optimization_barrier((mom_blocks, attended))
    own_mom = lax.all_to_all(mom_blocks, ("seq", "shard"), 0, 0).reshape(D, wide)
    column = lax.broadcasted_iota(jnp.int32, (D, wide), 1)
    is_out = s // owners == 1
    held = jnp.where(is_out & (column >= part_d // owners), 0.0, momentum_decay * own_mom.astype(f32) + own_grad)

    pieces = gather_seq_line(held.astype(b16), groups, z)
    grad_back = lax.all_to_all(
        own_grad_b.reshape(groups * shards, rows, wide), ("seq", "shard"), 0, 0
    )
    columns_here = jnp.concatenate(pieces, axis=1)
    gram = dot_nt(columns_here, columns_here)
    for b in range(owners.bit_length() - 1):
        mine = gram.astype(b16)
        gram = mine.astype(f32) + flip_shard(mine, shards, b).astype(f32)
    factor = 1.0 / (jnp.sqrt(jnp.trace(gram)) + 1e-07)

    def mul(x, y):
        return dot(x.astype(b16), y.astype(b16))

    a_zero = gram * (factor * factor)
    r_zero = cb * a_zero + cc * mul(a_zero, a_zero)
    r_zero_b = r_zero.astype(b16)
    once = ca * a_zero + mul(a_zero, r_zero_b)
    a_one = ca * once + mul(once, r_zero_b)
    a_one_b = a_one.astype(b16)
    r_one_b = (cb * a_one + cc * mul(a_one_b, a_one_b)).astype(b16)
    span = D // groups
    lead = lax.dynamic_slice_in_dim(a_one, z * span, span, 0)
    lead = ca * lead + mul(lead, r_one_b)
    lead = ca * lead + mul(lead, r_one_b)
    square = mul(lead, a_one_b)
    square = ca * square + mul(square, r_one_b)
    square = ca * square + mul(square, r_one_b)
    row_at = lax.broadcasted_iota(jnp.int32, (span, D), 0) + z * span
    unit = jnp.where(row_at == lax.broadcasted_iota(jnp.int32, (span, D), 1), ca, 0.0)
    last = unit + cb * lead + cc * square
    last = ca * last + mul(last, r_one_b)
    last = ca * last + mul(last, r_zero_b)
    last = (last * factor).astype(b16)
    result = dot(last, columns_here).astype(b16).reshape(shards, rows, groups * wide)
    result = lax.all_to_all(result, "shard", 0, 0)
    result = result.reshape(shards, rows, groups, wide)
    result = jnp.stack(
        [lax.dynamic_index_in_dim(result, (z - j) % groups, 2, False) for j in range(groups)], axis=2
    )
    ortho = result.reshape(4, owners, rows, groups, wide)
    grad_back = grad_back.reshape(groups, 4, owners, rows, wide)

    def rows_of(blocks, parts, width):
        cut = blocks[..., : width // groups // owners].reshape(rows, groups, parts, -1)
        return cut.transpose(0, 2, 1, 3).reshape(rows, width).astype(f32)

    widths = (3 * D, D, FF, FF)
    part_counts = (3, 1, 1, 1)
    weights = (w_qkv, w_out, w_up, w_down)
    moments = (mom_qkv, mom_out, mom_up, mom_down)
    grads, news, nexts = [], [], []
    for m in range(4):
        grad = rows_of(grad_back[:, m].transpose(2, 0, 1, 3), part_counts[m], widths[m])
        update = rows_of(ortho[m].transpose(1, 2, 0, 3), part_counts[m], widths[m])
        grads.append(grad)
        nexts.append(momentum_decay * moments[m] + grad)
        news.append(weights[m] - matrix_rate * 0.2 * math.sqrt(widths[m]) * update)
    grad_vec = jnp.sum(grad_back[:, 1, 0, 0, part_d // owners :].astype(f32), axis=0)
    next_vec = momentum_decay * mom_vectors + grad_vec
    new_vec = vectors - vector_rate / math.sqrt(total * shards) * next_vec
    return (
        block_rows[None],
        grad_rows[None],
        *grads,
        grad_vec,
        *news,
        new_vec,
        *nexts,
        next_vec,
    )


def solution(mesh):
    tokens = P("shard", "seq", None)
    matrix = P(("seq", "shard"), None)
    vector = P(("seq", "shard"))
    five = (matrix,) * 4 + (vector,)
    return jax.shard_map(
        per_device,
        mesh=mesh,
        in_specs=(tokens, tokens, P("shard", None)) + five + five,
        out_specs=(tokens, tokens) + five + five + five,
        check_vma=False,
    )
```

```python
import functools
import math

import jax
import jax.numpy as jnp
from jax import lax
from jax.experimental import pallas as pl
from jax.experimental.pallas import tpu as pltpu
from jax.sharding import PartitionSpec as P

D = 1024
H = 16
HD = 64
FF = 4096
VEC = 12 * D

ca, cb, cc = (3.4445, -4.775, 2.0315)
momentum_decay = 0.9
matrix_rate = 0.1
vector_rate = 0.2
f32 = jnp.float32
b16 = jnp.bfloat16


def layer_norm(values, gain_vec, shift_vec):
    center = values - jnp.mean(values, axis=-1, keepdims=True)
    spread = jnp.mean(center * center, axis=-1, keepdims=True)
    return center * lax.rsqrt(spread + 1e-05) * gain_vec + shift_vec


def normed(values):
    center = values - jnp.mean(values, axis=-1, keepdims=True)
    spread = jnp.mean(center * center, axis=-1, keepdims=True)
    return center * lax.rsqrt(spread + 1e-05)


def gelu_tanh(values):
    return jax.nn.gelu(values, approximate=True)


def dot(a, b):
    return jnp.dot(a, b, preferred_element_type=f32)


def dot_nt(a, b):
    return lax.dot_general(a, b, (((1,), (1,)), ((), ())), preferred_element_type=f32)


def dot_tn(a, b):
    return lax.dot_general(a, b, (((0,), (0,)), ((), ())), preferred_element_type=f32)


def lasting(microseconds):
    return pl.CostEstimate(
        flops=microseconds * 10**7, bytes_accessed=microseconds * 10**4, transcendentals=0
    )


def spans(total):
    rows = 128
    reach = total // 2
    out = []
    for begin in range(0, total, rows):
        first = max(0, begin - reach + 1) // 128 * 128
        out.append((begin, rows, first, begin + rows - first))
    return out


def probabilities(q, k, seg_q, seg_k, slope, offset):
    scores = dot_nt(q, k) * HD ** (-0.5)
    shape = scores.shape
    distance = offset + lax.broadcasted_iota(jnp.int32, shape, 0) - lax.broadcasted_iota(
        jnp.int32, shape, 1
    )
    scores = scores - slope * distance.astype(f32)
    scores = jnp.where((distance >= 0) & (seg_q == seg_k), scores, -1e30)
    terms = jnp.exp(scores - jnp.max(scores, axis=-1, keepdims=True))
    return terms * (1.0 / jnp.sum(terms, axis=-1, keepdims=True))


def attend_kernel(slopes, seg_col, seg_row, q, k, v, out):
    pair = pl.program_id(0)
    for j in range(2):
        cols = slice(j * HD, (j + 1) * HD)
        slope = slopes[2 * pair + j]
        for begin, rows, first, wide in spans(q.shape[0]):
            keys = slice(first, first + wide)
            probs = probabilities(
                q[begin : begin + rows, cols],
                k[keys, cols],
                seg_col[begin : begin + rows, :],
                seg_row[:, keys],
                slope,
                begin - first,
            )
            out[begin : begin + rows, cols] = dot(probs.astype(b16), v[keys, cols]).astype(b16)


def attend_back_kernel(slopes, seg_col, seg_row, q, k, v, g, dq, dk, dv, k_acc, v_acc):
    pair = pl.program_id(0)
    k_acc[...] = jnp.zeros_like(k_acc)
    v_acc[...] = jnp.zeros_like(v_acc)
    for j in range(2):
        cols = slice(j * HD, (j + 1) * HD)
        slope = slopes[2 * pair + j]
        for begin, rows, first, wide in spans(q.shape[0]):
            keys = slice(first, first + wide)
            q_block = q[begin : begin + rows, cols]
            g_block = g[begin : begin + rows, cols]
            probs = probabilities(
                q_block,
                k[keys, cols],
                seg_col[begin : begin + rows, :],
                seg_row[:, keys],
                slope,
                begin - first,
            )
            v_acc[keys, cols] += dot_tn(probs.astype(b16), g_block)
            grad_probs = dot_nt(g_block, v[keys, cols])
            inner = jnp.sum(probs * grad_probs, axis=-1, keepdims=True)
            grad_scores = (probs * (grad_probs - inner) * HD ** (-0.5)).astype(b16)
            dq[begin : begin + rows, cols] = dot(grad_scores, k[keys, cols]).astype(b16)
            k_acc[keys, cols] += dot_tn(grad_scores, q_block)
    dk[...] = k_acc[...].astype(b16)
    dv[...] = v_acc[...].astype(b16)


def attention_specs(total, pairs):
    col = pl.BlockSpec((total, 1), lambda p: (0, 0))
    row = pl.BlockSpec((1, total), lambda p: (0, 0))
    parts = [
        pl.BlockSpec((total, 2 * HD), lambda p, base=base: (0, base * pairs + p))
        for base in range(3)
    ]
    return [pl.BlockSpec(memory_space=pltpu.SMEM), col, row] + parts


def attend(slopes, seg, qkv, wide):
    total = qkv.shape[0]
    pairs = wide // (2 * HD)
    return pl.pallas_call(
        attend_kernel,
        grid=(pairs,),
        out_shape=jax.ShapeDtypeStruct((total, wide), b16),
        in_specs=attention_specs(total, pairs),
        out_specs=pl.BlockSpec((total, 2 * HD), lambda p: (0, p)),
        compiler_params=pltpu.CompilerParams(vmem_limit_bytes=24 * 2**20),
        cost_estimate=lasting(7),
    )(slopes, seg.reshape(total, 1), seg.reshape(1, total), qkv, qkv, qkv)


def attend_back(slopes, seg, qkv, grad, wide):
    total = qkv.shape[0]
    pairs = wide // (2 * HD)
    pair_spec = pl.BlockSpec((total, 2 * HD), lambda p: (0, p))
    part = jax.ShapeDtypeStruct((total, wide), b16)
    return pl.pallas_call(
        attend_back_kernel,
        grid=(pairs,),
        out_shape=(part, part, part),
        in_specs=attention_specs(total, pairs) + [pair_spec],
        out_specs=(pair_spec, pair_spec, pair_spec),
        scratch_shapes=[pltpu.VMEM((total, 2 * HD), f32), pltpu.VMEM((total, 2 * HD), f32)],
        compiler_params=pltpu.CompilerParams(vmem_limit_bytes=24 * 2**20),
        cost_estimate=lasting(11),
    )(slopes, seg.reshape(total, 1), seg.reshape(1, total), qkv, qkv, qkv, grad)


def gram_kernel(groups, place, *refs):
    blocks, (columns, gram) = refs[:-2], refs[-2:]
    each = 2 * groups - 1
    tall, wide = blocks[0].shape
    for part in range(len(blocks) // each):
        own, right, left = (
            blocks[part * each],
            blocks[part * each + 1 : part * each + groups],
            blocks[part * each + groups : (part + 1) * each],
        )
        at = slice(part * tall, (part + 1) * tall)
        columns[at, :wide] = own[...]
        for k in range(1, groups):
            cols = slice(k * wide, (k + 1) * wide)

            @pl.when(place[0] >= k)
            def _(source=right[k - 1], at=at, cols=cols):
                columns[at, cols] = source[...]

            @pl.when(place[0] < k)
            def _(source=left[groups - k - 1], at=at, cols=cols):
                columns[at, cols] = source[...]

    step = 256

    def one(i, carry):
        cut = pl.ds(i * step, step)
        gram[cut, :] = dot_nt(columns[cut, :], columns[...]).astype(b16)
        return carry

    lax.fori_loop(0, D // step, one, 0)


def gram_of(place, chunks, groups):
    blocks = [block for chunk in chunks for block in chunk]
    vmem = pl.BlockSpec(memory_space=pltpu.VMEM)
    wide = blocks[0].shape[1] * groups
    return pl.pallas_call(
        functools.partial(gram_kernel, groups),
        out_shape=(jax.ShapeDtypeStruct((D, wide), b16), jax.ShapeDtypeStruct((D, D), b16)),
        in_specs=[pl.BlockSpec(memory_space=pltpu.SMEM)] + [vmem] * len(blocks),
        out_specs=(vmem, vmem),
        compiler_params=pltpu.CompilerParams(vmem_limit_bytes=40 * 2**20),
        cost_estimate=lasting(8),
    )(place, *blocks)


def sweeps_kernel(place, mine, other, out, a_zero, a_zero_b, r_zero, a_one, a_one_b, r_one):
    step = 256
    span = out.shape[0]

    def blocks(body):
        def one(i, carry):
            body(pl.ds(i * step, step))
            return carry

        lax.fori_loop(0, D // step, one, 0)

    trace = jnp.zeros((1, 1), f32)
    for i in range(D // step):
        cut = slice(i * step, (i + 1) * step)
        gram = mine[cut, :].astype(f32) + other[cut, :].astype(f32)
        a_zero[cut, :] = gram
        at = lax.broadcasted_iota(jnp.int32, (step, D), 0) + i * step
        kept = jnp.where(at == lax.broadcasted_iota(jnp.int32, (step, D), 1), gram, 0.0)
        trace = trace + jnp.sum(jnp.sum(kept, axis=1, keepdims=True), axis=0, keepdims=True)
    factor = 1.0 / (jnp.sqrt(trace) + 1e-07)
    square_factor = factor * factor

    def scale(cut):
        scaled = a_zero[cut, :] * square_factor
        a_zero[cut, :] = scaled
        a_zero_b[cut, :] = scaled.astype(b16)

    def first(cut):
        r_zero[cut, :] = (cb * a_zero[cut, :] + cc * dot(a_zero_b[cut, :], a_zero_b[...])).astype(b16)

    def second(cut):
        once = ca * a_zero[cut, :] + dot(a_zero_b[cut, :], r_zero[...])
        twice = ca * once + dot(once.astype(b16), r_zero[...])
        a_one[cut, :] = twice
        a_one_b[cut, :] = twice.astype(b16)

    def third(cut):
        r_one[cut, :] = (cb * a_one[cut, :] + cc * dot(a_one_b[cut, :], a_one_b[...])).astype(b16)

    for body in (scale, first, second, third):
        blocks(body)
    begin = place[0] * span

    def by_p_one(values):
        return ca * values + dot(values.astype(b16), r_one[...])

    lead = by_p_one(by_p_one(a_one[pl.ds(begin, span), :]))
    square = by_p_one(by_p_one(dot(lead.astype(b16), a_one_b[...])))
    at = lax.broadcasted_iota(jnp.int32, (span, D), 0) + begin
    unit = jnp.where(at == lax.broadcasted_iota(jnp.int32, (span, D), 1), ca, 0.0)
    last = by_p_one(unit + cb * lead + cc * square)
    last = ca * last + dot(last.astype(b16), r_zero[...])
    out[...] = (last * factor).astype(b16)


def sweeps(place, mine, other, span):
    whole = pl.BlockSpec(memory_space=pltpu.VMEM)
    return pl.pallas_call(
        sweeps_kernel,
        out_shape=jax.ShapeDtypeStruct((span, D), b16),
        in_specs=[pl.BlockSpec(memory_space=pltpu.SMEM), whole, whole],
        out_specs=whole,
        scratch_shapes=[
            pltpu.VMEM((D, D), f32),
            pltpu.VMEM((D, D), b16),
            pltpu.VMEM((D, D), b16),
            pltpu.VMEM((D, D), f32),
            pltpu.VMEM((D, D), b16),
            pltpu.VMEM((D, D), b16),
        ],
        compiler_params=pltpu.CompilerParams(vmem_limit_bytes=40 * 2**20),
        cost_estimate=lasting(18),
    )(place, mine, other)


widths = (3 * D, D, FF, FF)
part_counts = (3, 1, 1, 1)


def column_runs(m, owners, groups, c):
    run = widths[m] // part_counts[m] // groups
    size = widths[m] // groups // owners
    out = []
    at = c * size
    while at < (c + 1) * size:
        part, inner = at // run, at % run
        count = min(run - inner, (c + 1) * size - at)
        out.append((at - c * size, part * (widths[m] // part_counts[m]) + inner, run, count))
        at += count
    return out


def aligned(owners, groups):
    return all(
        number % 128 == 0
        for m in range(4)
        for c in range(owners)
        for runs in column_runs(m, owners, groups, c)
        for number in runs
    )


def gradients_kernel(groups, owners, blocks, *refs):
    moments, grads, nexts = refs[:4], refs[4:8], refs[8:]
    for m in range(4):
        for c in range(owners):
            for z in range(groups):
                for inside, first, apart, count in column_runs(m, owners, groups, c):
                    cols = slice(first + z * apart, first + z * apart + count)
                    source = blocks[(z * 4 + m) * owners + c, :, inside : inside + count]
                    grad = source.astype(f32)
                    grads[m][:, cols] = grad
                    nexts[m][:, cols] = momentum_decay * moments[m][:, cols] + grad


def weights_kernel(groups, owners, place, blocks, *refs):
    weights, news = refs[:4], refs[4:]
    wide = blocks.shape[2] // groups
    for m in range(4):
        rate = matrix_rate * 0.2 * math.sqrt(widths[m])
        for c in range(owners):
            for k in range(groups):
                z = lax.rem(place[0] - k + groups, groups)
                for inside, first, apart, count in column_runs(m, owners, groups, c):
                    cols = pl.ds(pl.multiple_of(first + z * apart, 128), count)
                    begin = k * wide + inside
                    update = blocks[m * owners + c, :, begin : begin + count].astype(f32)
                    news[m][:, cols] = weights[m][:, cols] - rate * update


def shift_seq(array, groups, k):
    return lax.ppermute(array, "seq", [(i, (i + k) % groups) for i in range(groups)])


def flip_shard(array, shards, bit):
    return lax.ppermute(array, "shard", [(i, i ^ (1 << bit)) for i in range(shards)])


def rotations(array, groups):
    return [shift_seq(array, groups, k) for k in range(1, groups)]


def assemble(own, pieces, groups, z, axis):
    size = own.shape[axis]
    shape = list(own.shape)
    shape[axis] = size * groups
    full = jnp.zeros(shape, own.dtype)
    for k, piece in enumerate([own] + pieces):
        full = lax.dynamic_update_slice_in_dim(full, piece, (z - k) % groups * size, axis)
    return full


def gather_seq(array, groups, z, axis):
    return assemble(array, rotations(array, groups), groups, z, axis)


def exchange(blocks, groups, z):
    own = lax.dynamic_index_in_dim(blocks, z, 0, True)
    pieces = [
        shift_seq(lax.dynamic_index_in_dim(blocks, (z + k) % groups, 0, True), groups, k)
        for k in range(1, groups)
    ]
    return own, pieces


def reduce_start(array, groups, z):
    size = array.shape[0] // groups
    own = lax.dynamic_slice_in_dim(array, z * size, size, 0)
    pieces = []
    for k in range(1, groups):
        block = lax.dynamic_slice_in_dim(array, (z + k) % groups * size, size, 0)
        pieces.append(shift_seq(block.astype(b16), groups, k))
    return own, pieces


def line_seq(array, groups):
    right, left = [], []
    from_left = from_right = array
    for _ in range(groups - 1):
        from_left = lax.ppermute(from_left, "seq", [(i, i + 1) for i in range(groups - 1)])
        from_right = lax.ppermute(from_right, "seq", [(i + 1, i) for i in range(groups - 1)])
        right.append(from_left)
        left.append(from_right)
    return [array] + right + left


def per_device(
    tokens_in,
    out_grad,
    segments,
    w_qkv,
    w_out,
    w_up,
    w_down,
    vectors,
    mom_qkv,
    mom_out,
    mom_up,
    mom_down,
    mom_vectors,
):
    groups = lax.axis_size("seq")
    shards = lax.axis_size("shard")
    z = lax.axis_index("seq")
    s = lax.axis_index("shard")
    length = tokens_in.shape[1]
    total = length * groups
    rows = w_qkv.shape[0]
    owners = shards // 4
    part_d = D // groups
    part_f = FF // groups
    wide = part_f // owners
    chunk = vectors.shape[0]

    def columns_of(matrix, parts):
        split = matrix.astype(b16).reshape(rows, parts, groups, -1)
        return split.transpose(2, 0, 1, 3).reshape(groups, rows, -1)

    lanes = min(chunk, 128)
    vec_rows = chunk // lanes
    vec_block = jnp.pad(
        vectors.astype(b16).reshape(vec_rows, lanes), ((0, rows - vec_rows), (0, 128 - lanes))
    )
    send_a = jnp.concatenate(
        [columns_of(w_qkv, 3), jnp.broadcast_to(vec_block, (groups, rows, 128))], axis=2
    )
    got_a = assemble(*exchange(send_a, groups, z), groups, z, 0)
    all_a = lax.all_gather(got_a, "shard", axis=1).reshape(groups * shards, rows, -1)
    wide_qkv = all_a.reshape(D, -1)
    part_qkv = wide_qkv[:, : 3 * part_d]
    full_vec = all_a[:, :vec_rows, 3 * part_d : 3 * part_d + lanes].reshape(VEC).astype(f32).reshape(12, D)
    send_b = jnp.concatenate(
        [
            jnp.broadcast_to(w_out.astype(b16), (groups, rows, D)),
            columns_of(w_up, 1),
            columns_of(w_down, 1),
        ],
        axis=2,
    )
    send_b, _ = lax.optimization_barrier((send_b, got_a))
    got_b = assemble(*exchange(send_b, groups, z), groups, z, 0)
    own_tokens, got_b = lax.optimization_barrier((tokens_in[0], got_b))
    all_b = lax.all_gather(got_b, "shard", axis=1).reshape(D, -1)
    full_out = all_b[:, :D]
    part_up = all_b[:, D : D + part_f]
    part_down = all_b[:, D + part_f :]
    pieces_tokens = rotations(own_tokens, groups)
    def blocks_of(matrix, parts):
        split = matrix.astype(b16).reshape(rows, parts, groups, -1).transpose(0, 2, 1, 3)
        split = split.reshape(rows, groups, owners, -1)
        return jnp.pad(split, ((0, 0), (0, 0), (0, 0), (0, wide - split.shape[3])))

    mom_blocks = jnp.stack(
        [
            blocks_of(moment, parts)
            for moment, parts in zip((mom_qkv, mom_out, mom_up, mom_down), part_counts)
        ]
    )
    mom_blocks = mom_blocks.transpose(0, 3, 2, 1, 4).reshape(shards, groups, rows, wide)
    mom_blocks, _ = lax.optimization_barrier((mom_blocks, got_b))
    mom_rows = lax.all_to_all(mom_blocks, "shard", 0, 0)
    mom_rows = mom_rows.transpose(1, 0, 2, 3).reshape(groups, shards * rows, wide)
    pieces_tokens, own_cotangent = lax.optimization_barrier((pieces_tokens, out_grad[0]))
    pieces_cotangent = rotations(own_cotangent, groups)
    tokens_all = assemble(own_tokens, pieces_tokens, groups, z, 0)
    residual = tokens_all.astype(f32)

    gain_one, shift_one, bias_query, bias_value, bias_out, gain_two, shift_two = (
        full_vec[i] for i in range(7)
    )
    bias_up = lax.dynamic_slice_in_dim(full_vec[7:11].reshape(FF), z * part_f, part_f, 0)
    bias_down = full_vec[11]
    part_bias = jnp.concatenate(
        [
            lax.dynamic_slice_in_dim(bias_query, z * part_d, part_d, 0),
            jnp.zeros((part_d,), f32),
            lax.dynamic_slice_in_dim(bias_value, z * part_d, part_d, 0),
            jnp.zeros((128,), f32),
        ]
    )

    normed_one = normed(residual)
    hidden_one = (normed_one * gain_one + shift_one).astype(b16)
    qkv = (dot(hidden_one, wide_qkv) + part_bias).astype(b16)
    head_count = part_d // HD
    heads = (z * head_count + jnp.arange(head_count)).astype(f32)
    slopes = jnp.exp2(-8.0 * (heads + 1.0) / H)
    attended_part = attend(slopes, segments[0], qkv, part_d)
    pieces_cotangent, attended_part = lax.optimization_barrier((pieces_cotangent, attended_part))
    pieces_attended = rotations(attended_part, groups)
    attended = assemble(attended_part, pieces_attended, groups, z, 1)

    middle = residual + dot(attended, full_out) + bias_out
    normed_two = normed(middle)
    hidden_two = (normed_two * gain_two + shift_two).astype(b16)
    before = dot(hidden_two, part_up) + bias_up
    active_wide, gelu_back = jax.vjp(gelu_tanh, before)
    active = active_wide.astype(b16)
    gelu_slope = gelu_back(jnp.ones_like(before))[0]
    own_upstream = out_grad[0].astype(f32)

    low = s & 1

    def core_sum(left, right, padded):
        size = right.shape[1] // owners

        def half(bit):
            cuts = [
                lax.dynamic_slice_in_dim(right, (2 * high + bit) * size, size, 1)
                for high in range(owners // 2)
            ]
            return jnp.stack([dot_tn(left, cut).astype(b16) for cut in cuts])

        got = flip_shard(half(1 - low), shards, 0)
        both = (half(low).astype(f32) + got.astype(f32)).astype(b16)
        return jnp.pad(both, ((0, 0), (0, 0), (0, padded - size)))

    top = shards.bit_length() - 2
    inner = list(range(1, top - 1))

    def over_shard(four):
        stacked = jnp.stack(four)
        stacked = stacked.reshape([2] * (2 + len(inner)) + list(stacked.shape[2:]))
        sums = []
        for part, order in (
            (stacked[..., : D // 2, :], inner + [top - 1, top]),
            (stacked[..., D // 2 :, :], [top] + inner + [top - 1]),
        ):
            left = [top, top - 1] + inner[::-1]
            for b in order:
                ax = left.index(b)
                left.pop(ax)
                mine = (s >> b) & 1
                keep = lax.dynamic_index_in_dim(part, mine, ax, False)
                give = lax.dynamic_index_in_dim(part, 1 - mine, ax, False)
                got = flip_shard(give, shards, b)
                part = keep.astype(f32) + got.astype(f32)
                if left:
                    part = part.astype(b16)
            sums.append(part)
        return sums

    gelu_slope, pieces_cotangent = lax.optimization_barrier((gelu_slope, pieces_cotangent))
    cotangent = assemble(own_cotangent, pieces_cotangent, groups, z, 0)
    grad_before = dot(cotangent, part_down) * gelu_slope
    grad_before_b = grad_before.astype(b16)
    hidden_two_share = dot_nt(grad_before_b, part_up)
    own_share, pieces = reduce_start(hidden_two_share, groups, z)
    sum_up = core_sum(hidden_two, grad_before_b, wide)
    block_share = dot_nt(active, part_down)
    pieces, sum_up, block_share = lax.optimization_barrier((pieces, sum_up, block_share))
    grad_hidden_two = own_share + sum(piece.astype(f32) for piece in pieces)
    own_middle = lax.dynamic_slice_in_dim(middle, z * length, length, 0)
    middle_part = jax.vjp(lambda m: layer_norm(m, gain_two, shift_two), own_middle)[1](
        grad_hidden_two
    )[0]
    grad_middle = own_upstream + middle_part
    grad_middle_b = grad_middle.astype(b16)
    grad_attended = dot_nt(grad_middle_b, full_out).astype(b16)

    columns_sent = jnp.concatenate(
        [array.reshape(length, groups, part_d) for array in (grad_attended, grad_middle_b)], axis=2
    )
    head_grad = lax.all_to_all(columns_sent.transpose(1, 0, 2), "seq", 0, 0)
    head_grad = head_grad.reshape(total, 2 * part_d)
    sum_down = core_sum(cotangent, active, wide)
    head_grad, sum_down, block_share = lax.optimization_barrier((head_grad, sum_down, block_share))
    middle_cols = head_grad[:, part_d:]

    grad_q, grad_k, grad_v = attend_back(slopes, segments[0], qkv, head_grad, part_d)
    grad_mixed = jnp.concatenate([grad_q, grad_k, grad_v], axis=1)

    mom_rows, grad_mixed = lax.optimization_barrier((mom_rows, grad_mixed))
    own_mom = lax.all_to_all(mom_rows, "seq", 0, 0).reshape(D, wide)
    halves = over_shard(
        [core_sum(hidden_one, grad_mixed, wide), core_sum(attended, middle_cols, wide), sum_up, sum_down]
    )
    own_grad_b = jnp.concatenate(halves, axis=0).astype(b16)
    held = [
        (momentum_decay * mom.astype(f32) + grad).astype(b16)
        for mom, grad in zip((own_mom[: D // 2], own_mom[D // 2 :]), halves)
    ]

    held[1], hidden_two_share, late_mixed = lax.optimization_barrier(
        (held[1], hidden_two_share, grad_mixed)
    )
    hidden_one_share = dot_nt(late_mixed, part_qkv)
    def placed(values, width):
        return lax.dynamic_update_slice_in_dim(jnp.zeros((width,), f32), values, z * values.shape[0], 0)

    share_vec = jnp.concatenate(
        [
            jnp.sum(hidden_one_share * normed_one, axis=0),
            jnp.sum(hidden_one_share, axis=0),
            placed(jnp.sum(late_mixed[:, :part_d].astype(f32), axis=0), D),
            placed(jnp.sum(late_mixed[:, 2 * part_d :].astype(f32), axis=0), D),
            jnp.sum(grad_middle, axis=0),
            jnp.sum(hidden_two_share * normed_two, axis=0),
            jnp.sum(hidden_two_share, axis=0),
            placed(jnp.sum(grad_before, axis=0), FF),
            jnp.sum(own_upstream, axis=0),
        ]
    )
    chunks = [line_seq(cut, groups) for cut in held]
    chunks, hidden_one_share, share_vec = lax.optimization_barrier(
        (chunks, hidden_one_share, share_vec)
    )
    place = z.reshape(1)
    columns_here, gram = gram_of(place, chunks, groups)
    own_grad_b, gram = lax.optimization_barrier((own_grad_b, gram))
    other = flip_shard(gram, shards, 0)
    for b in range(1, owners.bit_length() - 1):
        gram = (gram.astype(f32) + other.astype(f32)).astype(b16)
        other = flip_shard(gram, shards, b)
    grad_back = lax.all_to_all(
        own_grad_b.reshape(groups * shards, rows, wide), ("seq", "shard"), 0, 0
    )
    last = sweeps(place, gram, other, D // groups)
    own_one, one_others = reduce_start(hidden_one_share, groups, z)
    last, one_others, block_share = lax.optimization_barrier((last, one_others, block_share))
    own_block, block_others = reduce_start(block_share, groups, z)
    result = dot(last, columns_here).astype(b16).reshape(shards, rows, groups * wide)
    result = lax.all_to_all(result, "shard", 0, 0)
    result, grad_back, share_vec, block_others = lax.optimization_barrier(
        (result, grad_back, share_vec, block_others)
    )
    vec_back = lax.all_to_all(share_vec.reshape(groups * shards, 1, chunk), ("seq", "shard"), 0, 0)
    grad_hidden_one = own_one + sum(piece.astype(f32) for piece in one_others)
    block_sum = own_block + sum(piece.astype(f32) for piece in block_others)
    block_rows = (block_sum + own_middle + bias_down).astype(b16)
    own_residual = tokens_in[0].astype(f32)
    input_part = jax.vjp(lambda m: layer_norm(m, gain_one, shift_one), own_residual)[1](
        grad_hidden_one
    )[0]
    grad_rows = grad_middle + input_part

    weights = (w_qkv, w_out, w_up, w_down)
    moments = (mom_qkv, mom_out, mom_up, mom_down)
    if aligned(owners, groups):
        vmem = pl.BlockSpec(memory_space=pltpu.VMEM)
        four = tuple(jax.ShapeDtypeStruct((rows, w), f32) for w in widths)
        params = pltpu.CompilerParams(vmem_limit_bytes=24 * 2**20)
        both = pl.pallas_call(
            functools.partial(gradients_kernel, groups, owners),
            out_shape=four + four,
            in_specs=[vmem] * 5,
            out_specs=(vmem,) * 8,
            compiler_params=params,
        )(grad_back, *moments)
        grads, nexts = both[:4], both[4:]
        news = pl.pallas_call(
            functools.partial(weights_kernel, groups, owners),
            out_shape=four,
            in_specs=[pl.BlockSpec(memory_space=pltpu.SMEM)] + [vmem] * 5,
            out_specs=(vmem,) * 4,
            compiler_params=params,
        )(place, result, *weights)
    else:
        result = result.reshape(shards, rows, groups, wide)
        result = jnp.stack(
            [
                lax.dynamic_index_in_dim(result, (z - j) % groups, 2, False)
                for j in range(groups)
            ],
            axis=2,
        )
        ortho = result.reshape(4, owners, rows, groups, wide)
        grad_blocks = grad_back.reshape(groups, 4, owners, rows, wide)

        def rows_of(blocks, parts, width):
            cut = blocks[..., : width // groups // owners].reshape(rows, groups, parts, -1)
            return cut.transpose(0, 2, 1, 3).reshape(rows, width).astype(f32)

        grads, news, nexts = [], [], []
        for m in range(4):
            grad = rows_of(grad_blocks[:, m].transpose(2, 0, 1, 3), part_counts[m], widths[m])
            update = rows_of(ortho[m].transpose(1, 2, 0, 3), part_counts[m], widths[m])
            grads.append(grad)
            nexts.append(momentum_decay * moments[m] + grad)
            news.append(weights[m] - matrix_rate * 0.2 * math.sqrt(widths[m]) * update)
    grad_vec = jnp.sum(vec_back, axis=(0, 1))
    next_vec = momentum_decay * mom_vectors + grad_vec
    new_vec = vectors - vector_rate / math.sqrt(total * shards) * next_vec
    return (
        block_rows[None],
        grad_rows[None],
        *grads,
        grad_vec,
        *news,
        new_vec,
        *nexts,
        next_vec,
    )


def solution(mesh):
    tokens = P("shard", "seq", None)
    matrix = P(("seq", "shard"), None)
    vector = P(("seq", "shard"))
    five = (matrix,) * 4 + (vector,)
    return jax.shard_map(
        per_device,
        mesh=mesh,
        in_specs=(tokens, tokens, P("shard", None)) + five + five,
        out_specs=(tokens, tokens) + five + five + five,
        check_vma=False,
    )
```

```python
import functools
import math

import jax
import jax.numpy as jnp
from jax import lax
from jax.experimental import pallas as pl
from jax.experimental.pallas import tpu as pltpu
from jax.sharding import PartitionSpec as P

D = 1024
H = 16
HD = 64
FF = 4096
VEC = 12 * D

ca, cb, cc = (3.4445, -4.775, 2.0315)
momentum_decay = 0.9
matrix_rate = 0.1
vector_rate = 0.2
f32 = jnp.float32
b16 = jnp.bfloat16


def layer_norm(values, gain_vec, shift_vec):
    center = values - jnp.mean(values, axis=-1, keepdims=True)
    spread = jnp.mean(center * center, axis=-1, keepdims=True)
    return center * lax.rsqrt(spread + 1e-05) * gain_vec + shift_vec


def normed(values):
    center = values - jnp.mean(values, axis=-1, keepdims=True)
    spread = jnp.mean(center * center, axis=-1, keepdims=True)
    return center * lax.rsqrt(spread + 1e-05)


def gelu_tanh(values):
    return jax.nn.gelu(values, approximate=True)


def dot(a, b):
    return jnp.dot(a, b, preferred_element_type=f32)


def dot_nt(a, b):
    return lax.dot_general(a, b, (((1,), (1,)), ((), ())), preferred_element_type=f32)


def dot_tn(a, b):
    return lax.dot_general(a, b, (((0,), (0,)), ((), ())), preferred_element_type=f32)


def lasting(microseconds):
    return pl.CostEstimate(
        flops=microseconds * 10**7, bytes_accessed=microseconds * 10**4, transcendentals=0
    )


def spans(total):
    rows = 128
    reach = total // 2
    out = []
    for begin in range(0, total, rows):
        first = max(0, begin - reach + 1) // 128 * 128
        out.append((begin, rows, first, begin + rows - first))
    return out


def probabilities(q, k, seg_q, seg_k, slope, offset):
    scores = dot_nt(q, k) * HD ** (-0.5)
    shape = scores.shape
    distance = offset + lax.broadcasted_iota(jnp.int32, shape, 0) - lax.broadcasted_iota(
        jnp.int32, shape, 1
    )
    scores = scores - slope * distance.astype(f32)
    scores = jnp.where((distance >= 0) & (seg_q == seg_k), scores, -1e30)
    terms = jnp.exp(scores - jnp.max(scores, axis=-1, keepdims=True))
    return terms * (1.0 / jnp.sum(terms, axis=-1, keepdims=True))


def attend_kernel(slopes, seg_col, seg_row, q, k, v, out):
    pair = pl.program_id(0)
    for j in range(2):
        cols = slice(j * HD, (j + 1) * HD)
        slope = slopes[2 * pair + j]
        for begin, rows, first, wide in spans(q.shape[0]):
            keys = slice(first, first + wide)
            probs = probabilities(
                q[begin : begin + rows, cols],
                k[keys, cols],
                seg_col[begin : begin + rows, :],
                seg_row[:, keys],
                slope,
                begin - first,
            )
            out[begin : begin + rows, cols] = dot(probs.astype(b16), v[keys, cols]).astype(b16)


def attend_back_kernel(slopes, seg_col, seg_row, q, k, v, g, dq, dk, dv, k_acc, v_acc):
    pair = pl.program_id(0)
    k_acc[...] = jnp.zeros_like(k_acc)
    v_acc[...] = jnp.zeros_like(v_acc)
    for j in range(2):
        cols = slice(j * HD, (j + 1) * HD)
        slope = slopes[2 * pair + j]
        for begin, rows, first, wide in spans(q.shape[0]):
            keys = slice(first, first + wide)
            q_block = q[begin : begin + rows, cols]
            g_block = g[begin : begin + rows, cols]
            probs = probabilities(
                q_block,
                k[keys, cols],
                seg_col[begin : begin + rows, :],
                seg_row[:, keys],
                slope,
                begin - first,
            )
            v_acc[keys, cols] += dot_tn(probs.astype(b16), g_block)
            grad_probs = dot_nt(g_block, v[keys, cols])
            inner = jnp.sum(probs * grad_probs, axis=-1, keepdims=True)
            grad_scores = (probs * (grad_probs - inner) * HD ** (-0.5)).astype(b16)
            dq[begin : begin + rows, cols] = dot(grad_scores, k[keys, cols]).astype(b16)
            k_acc[keys, cols] += dot_tn(grad_scores, q_block)
    dk[...] = k_acc[...].astype(b16)
    dv[...] = v_acc[...].astype(b16)


def attention_specs(total, pairs):
    col = pl.BlockSpec((total, 1), lambda p: (0, 0))
    row = pl.BlockSpec((1, total), lambda p: (0, 0))
    parts = [
        pl.BlockSpec((total, 2 * HD), lambda p, base=base: (0, base * pairs + p))
        for base in range(3)
    ]
    return [pl.BlockSpec(memory_space=pltpu.SMEM), col, row] + parts


def attend(slopes, seg, qkv, wide):
    total = qkv.shape[0]
    pairs = wide // (2 * HD)
    return pl.pallas_call(
        attend_kernel,
        grid=(pairs,),
        out_shape=jax.ShapeDtypeStruct((total, wide), b16),
        in_specs=attention_specs(total, pairs),
        out_specs=pl.BlockSpec((total, 2 * HD), lambda p: (0, p)),
        compiler_params=pltpu.CompilerParams(vmem_limit_bytes=24 * 2**20),
        cost_estimate=lasting(7),
    )(slopes, seg.reshape(total, 1), seg.reshape(1, total), qkv, qkv, qkv)


def attend_back(slopes, seg, qkv, grad, wide):
    total = qkv.shape[0]
    pairs = wide // (2 * HD)
    pair_spec = pl.BlockSpec((total, 2 * HD), lambda p: (0, p))
    part = jax.ShapeDtypeStruct((total, wide), b16)
    return pl.pallas_call(
        attend_back_kernel,
        grid=(pairs,),
        out_shape=(part, part, part),
        in_specs=attention_specs(total, pairs) + [pair_spec],
        out_specs=(pair_spec, pair_spec, pair_spec),
        scratch_shapes=[pltpu.VMEM((total, 2 * HD), f32), pltpu.VMEM((total, 2 * HD), f32)],
        compiler_params=pltpu.CompilerParams(vmem_limit_bytes=24 * 2**20),
        cost_estimate=lasting(11),
    )(slopes, seg.reshape(total, 1), seg.reshape(1, total), qkv, qkv, qkv, grad)


def gram_kernel(groups, place, *refs):
    blocks, (columns, gram) = refs[:-2], refs[-2:]
    each = 2 * groups - 1
    tall, wide = blocks[0].shape
    for part in range(len(blocks) // each):
        own, right, left = (
            blocks[part * each],
            blocks[part * each + 1 : part * each + groups],
            blocks[part * each + groups : (part + 1) * each],
        )
        at = slice(part * tall, (part + 1) * tall)
        columns[at, :wide] = own[...]
        for k in range(1, groups):
            cols = slice(k * wide, (k + 1) * wide)

            @pl.when(place[0] >= k)
            def _(source=right[k - 1], at=at, cols=cols):
                columns[at, cols] = source[...]

            @pl.when(place[0] < k)
            def _(source=left[groups - k - 1], at=at, cols=cols):
                columns[at, cols] = source[...]

    step = 256

    def one(i, carry):
        cut = pl.ds(i * step, step)
        gram[cut, :] = dot_nt(columns[cut, :], columns[...]).astype(b16)
        return carry

    lax.fori_loop(0, D // step, one, 0)


def gram_of(place, chunks, groups):
    blocks = [block for chunk in chunks for block in chunk]
    vmem = pl.BlockSpec(memory_space=pltpu.VMEM)
    wide = blocks[0].shape[1] * groups
    return pl.pallas_call(
        functools.partial(gram_kernel, groups),
        out_shape=(jax.ShapeDtypeStruct((D, wide), b16), jax.ShapeDtypeStruct((D, D), b16)),
        in_specs=[pl.BlockSpec(memory_space=pltpu.SMEM)] + [vmem] * len(blocks),
        out_specs=(vmem, vmem),
        compiler_params=pltpu.CompilerParams(vmem_limit_bytes=40 * 2**20),
        cost_estimate=lasting(8),
    )(place, *blocks)


def sweeps_kernel(place, mine, other, out, a_zero, a_zero_b, r_zero, a_one, a_one_b, r_one):
    step = 256
    span = out.shape[0]

    def blocks(body):
        def one(i, carry):
            body(pl.ds(i * step, step))
            return carry

        lax.fori_loop(0, D // step, one, 0)

    trace = jnp.zeros((1, 1), f32)
    for i in range(D // step):
        cut = slice(i * step, (i + 1) * step)
        gram = mine[cut, :].astype(f32) + other[cut, :].astype(f32)
        a_zero[cut, :] = gram
        at = lax.broadcasted_iota(jnp.int32, (step, D), 0) + i * step
        kept = jnp.where(at == lax.broadcasted_iota(jnp.int32, (step, D), 1), gram, 0.0)
        trace = trace + jnp.sum(jnp.sum(kept, axis=1, keepdims=True), axis=0, keepdims=True)
    factor = 1.0 / (jnp.sqrt(trace) + 1e-07)
    square_factor = factor * factor

    def scale(cut):
        scaled = a_zero[cut, :] * square_factor
        a_zero[cut, :] = scaled
        a_zero_b[cut, :] = scaled.astype(b16)

    def first(cut):
        r_zero[cut, :] = (cb * a_zero[cut, :] + cc * dot(a_zero_b[cut, :], a_zero_b[...])).astype(b16)

    def second(cut):
        once = ca * a_zero[cut, :] + dot(a_zero_b[cut, :], r_zero[...])
        twice = ca * once + dot(once.astype(b16), r_zero[...])
        a_one[cut, :] = twice
        a_one_b[cut, :] = twice.astype(b16)

    def third(cut):
        r_one[cut, :] = (cb * a_one[cut, :] + cc * dot(a_one_b[cut, :], a_one_b[...])).astype(b16)

    for body in (scale, first, second, third):
        blocks(body)
    begin = place[0] * span

    def by_p_one(values):
        return ca * values + dot(values.astype(b16), r_one[...])

    lead = by_p_one(by_p_one(a_one[pl.ds(begin, span), :]))
    square = by_p_one(by_p_one(dot(lead.astype(b16), a_one_b[...])))
    at = lax.broadcasted_iota(jnp.int32, (span, D), 0) + begin
    unit = jnp.where(at == lax.broadcasted_iota(jnp.int32, (span, D), 1), ca, 0.0)
    last = by_p_one(unit + cb * lead + cc * square)
    last = ca * last + dot(last.astype(b16), r_zero[...])
    out[...] = (last * factor).astype(b16)


def sweeps(place, mine, other, span):
    whole = pl.BlockSpec(memory_space=pltpu.VMEM)
    return pl.pallas_call(
        sweeps_kernel,
        out_shape=jax.ShapeDtypeStruct((span, D), b16),
        in_specs=[pl.BlockSpec(memory_space=pltpu.SMEM), whole, whole],
        out_specs=whole,
        scratch_shapes=[
            pltpu.VMEM((D, D), f32),
            pltpu.VMEM((D, D), b16),
            pltpu.VMEM((D, D), b16),
            pltpu.VMEM((D, D), f32),
            pltpu.VMEM((D, D), b16),
            pltpu.VMEM((D, D), b16),
        ],
        compiler_params=pltpu.CompilerParams(vmem_limit_bytes=40 * 2**20),
        cost_estimate=lasting(18),
    )(place, mine, other)


widths = (3 * D, D, FF, FF)
part_counts = (3, 1, 1, 1)


def column_runs(m, owners, groups, c):
    run = widths[m] // part_counts[m] // groups
    size = widths[m] // groups // owners
    out = []
    at = c * size
    while at < (c + 1) * size:
        part, inner = at // run, at % run
        count = min(run - inner, (c + 1) * size - at)
        out.append((at - c * size, part * (widths[m] // part_counts[m]) + inner, run, count))
        at += count
    return out


def aligned(owners, groups):
    return all(
        number % 128 == 0
        for m in range(4)
        for c in range(owners)
        for runs in column_runs(m, owners, groups, c)
        for number in runs
    )


def gradients_kernel(groups, owners, blocks, *refs):
    moments, grads, nexts = refs[:4], refs[4:8], refs[8:]
    for m in range(4):
        for c in range(owners):
            for z in range(groups):
                for inside, first, apart, count in column_runs(m, owners, groups, c):
                    cols = slice(first + z * apart, first + z * apart + count)
                    source = blocks[(z * 4 + m) * owners + c, :, inside : inside + count]
                    grad = source.astype(f32)
                    grads[m][:, cols] = grad
                    nexts[m][:, cols] = momentum_decay * moments[m][:, cols] + grad


def weights_kernel(groups, owners, place, blocks, *refs):
    weights, news = refs[:4], refs[4:]
    wide = blocks.shape[2] // groups
    for m in range(4):
        rate = matrix_rate * 0.2 * math.sqrt(widths[m])
        for c in range(owners):
            for k in range(groups):
                z = lax.rem(place[0] - k + groups, groups)
                for inside, first, apart, count in column_runs(m, owners, groups, c):
                    cols = pl.ds(pl.multiple_of(first + z * apart, 128), count)
                    begin = k * wide + inside
                    update = blocks[m * owners + c, :, begin : begin + count].astype(f32)
                    news[m][:, cols] = weights[m][:, cols] - rate * update


def shift_seq(array, groups, k):
    return lax.ppermute(array, "seq", [(i, (i + k) % groups) for i in range(groups)])


def flip_shard(array, shards, bit):
    return lax.ppermute(array, "shard", [(i, i ^ (1 << bit)) for i in range(shards)])


def rotations(array, groups):
    return [shift_seq(array, groups, k) for k in range(1, groups)]


def assemble(own, pieces, groups, z, axis):
    size = own.shape[axis]
    shape = list(own.shape)
    shape[axis] = size * groups
    full = jnp.zeros(shape, own.dtype)
    for k, piece in enumerate([own] + pieces):
        full = lax.dynamic_update_slice_in_dim(full, piece, (z - k) % groups * size, axis)
    return full


def gather_seq(array, groups, z, axis):
    return assemble(array, rotations(array, groups), groups, z, axis)


def exchange(blocks, groups, z):
    own = lax.dynamic_index_in_dim(blocks, z, 0, True)
    pieces = [
        shift_seq(lax.dynamic_index_in_dim(blocks, (z + k) % groups, 0, True), groups, k)
        for k in range(1, groups)
    ]
    return own, pieces


def reduce_start(array, groups, z):
    size = array.shape[0] // groups
    own = lax.dynamic_slice_in_dim(array, z * size, size, 0)
    pieces = []
    for k in range(1, groups):
        block = lax.dynamic_slice_in_dim(array, (z + k) % groups * size, size, 0)
        pieces.append(shift_seq(block.astype(b16), groups, k))
    return own, pieces


def line_seq(array, groups):
    right, left = [], []
    from_left = from_right = array
    for _ in range(groups - 1):
        from_left = lax.ppermute(from_left, "seq", [(i, i + 1) for i in range(groups - 1)])
        from_right = lax.ppermute(from_right, "seq", [(i + 1, i) for i in range(groups - 1)])
        right.append(from_left)
        left.append(from_right)
    return [array] + right + left


def per_device(
    tokens_in,
    out_grad,
    segments,
    w_qkv,
    w_out,
    w_up,
    w_down,
    vectors,
    mom_qkv,
    mom_out,
    mom_up,
    mom_down,
    mom_vectors,
):
    groups = lax.axis_size("seq")
    shards = lax.axis_size("shard")
    z = lax.axis_index("seq")
    s = lax.axis_index("shard")
    length = tokens_in.shape[1]
    total = length * groups
    rows = w_qkv.shape[0]
    owners = shards // 4
    part_d = D // groups
    part_f = FF // groups
    wide = part_f // owners
    chunk = vectors.shape[0]

    def columns_of(matrix, parts):
        split = matrix.astype(b16).reshape(rows, parts, groups, -1)
        return split.transpose(2, 0, 1, 3).reshape(groups, rows, -1)

    lanes = min(chunk, 128)
    vec_rows = chunk // lanes
    vec_block = jnp.pad(
        vectors.astype(b16).reshape(vec_rows, lanes), ((0, rows - vec_rows), (0, 128 - lanes))
    )
    send_a = jnp.concatenate(
        [columns_of(w_qkv, 3), jnp.broadcast_to(vec_block, (groups, rows, 128))], axis=2
    )
    got_a = assemble(*exchange(send_a, groups, z), groups, z, 0)
    all_a = lax.all_gather(got_a, "shard", axis=1).reshape(groups * shards, rows, -1)
    wide_qkv = all_a.reshape(D, -1)
    part_qkv = wide_qkv[:, : 3 * part_d]
    full_vec = all_a[:, :vec_rows, 3 * part_d : 3 * part_d + lanes].reshape(VEC).astype(f32).reshape(12, D)
    send_b = jnp.concatenate(
        [
            jnp.broadcast_to(w_out.astype(b16), (groups, rows, D)),
            columns_of(w_up, 1),
            columns_of(w_down, 1),
        ],
        axis=2,
    )
    send_b, _ = lax.optimization_barrier((send_b, got_a))
    got_b = lax.all_to_all(send_b, "seq", 0, 0)
    own_tokens, got_b = lax.optimization_barrier((tokens_in[0], got_b))
    all_b = lax.all_gather(got_b, "shard", axis=1).reshape(D, -1)
    full_out = all_b[:, :D]
    part_up = all_b[:, D : D + part_f]
    part_down = all_b[:, D + part_f :]
    pieces_tokens = rotations(own_tokens, groups)
    def blocks_of(matrix, parts):
        split = matrix.astype(b16).reshape(rows, parts, groups, -1).transpose(0, 2, 1, 3)
        split = split.reshape(rows, groups, owners, -1)
        return jnp.pad(split, ((0, 0), (0, 0), (0, 0), (0, wide - split.shape[3])))

    mom_blocks = jnp.stack(
        [
            blocks_of(moment, parts)
            for moment, parts in zip((mom_qkv, mom_out, mom_up, mom_down), part_counts)
        ]
    )
    mom_blocks = mom_blocks.transpose(0, 3, 2, 1, 4).reshape(shards, groups, rows, wide)
    mom_blocks, _ = lax.optimization_barrier((mom_blocks, got_b))
    mom_rows = lax.all_to_all(mom_blocks, "shard", 0, 0)
    mom_rows = mom_rows.transpose(1, 0, 2, 3).reshape(groups, shards * rows, wide)
    pieces_tokens, own_cotangent = lax.optimization_barrier((pieces_tokens, out_grad[0]))
    pieces_cotangent = rotations(own_cotangent, groups)
    tokens_all = assemble(own_tokens, pieces_tokens, groups, z, 0)
    residual = tokens_all.astype(f32)

    gain_one, shift_one, bias_query, bias_value, bias_out, gain_two, shift_two = (
        full_vec[i] for i in range(7)
    )
    bias_up = lax.dynamic_slice_in_dim(full_vec[7:11].reshape(FF), z * part_f, part_f, 0)
    bias_down = full_vec[11]
    part_bias = jnp.concatenate(
        [
            lax.dynamic_slice_in_dim(bias_query, z * part_d, part_d, 0),
            jnp.zeros((part_d,), f32),
            lax.dynamic_slice_in_dim(bias_value, z * part_d, part_d, 0),
            jnp.zeros((128,), f32),
        ]
    )

    normed_one = normed(residual)
    hidden_one = (normed_one * gain_one + shift_one).astype(b16)
    qkv = (dot(hidden_one, wide_qkv) + part_bias).astype(b16)
    head_count = part_d // HD
    heads = (z * head_count + jnp.arange(head_count)).astype(f32)
    slopes = jnp.exp2(-8.0 * (heads + 1.0) / H)
    attended_part = attend(slopes, segments[0], qkv, part_d)
    pieces_cotangent, attended_part = lax.optimization_barrier((pieces_cotangent, attended_part))
    pieces_attended = rotations(attended_part, groups)
    attended = assemble(attended_part, pieces_attended, groups, z, 1)

    middle = residual + dot(attended, full_out) + bias_out
    normed_two = normed(middle)
    hidden_two = (normed_two * gain_two + shift_two).astype(b16)
    before = dot(hidden_two, part_up) + bias_up
    active_wide, gelu_back = jax.vjp(gelu_tanh, before)
    active = active_wide.astype(b16)
    gelu_slope = gelu_back(jnp.ones_like(before))[0]
    own_upstream = out_grad[0].astype(f32)

    low = s & 1

    def core_sum(left, right, padded):
        size = right.shape[1] // owners

        def half(bit):
            cuts = [
                lax.dynamic_slice_in_dim(right, (2 * high + bit) * size, size, 1)
                for high in range(owners // 2)
            ]
            return jnp.stack([dot_tn(left, cut).astype(b16) for cut in cuts])

        got = flip_shard(half(1 - low), shards, 0)
        both = (half(low).astype(f32) + got.astype(f32)).astype(b16)
        return jnp.pad(both, ((0, 0), (0, 0), (0, padded - size)))

    top = shards.bit_length() - 2
    inner = list(range(1, top - 1))

    def over_shard(four):
        stacked = jnp.stack(four)
        stacked = stacked.reshape([2] * (2 + len(inner)) + list(stacked.shape[2:]))
        sums = []
        for part, order in (
            (stacked[..., : D // 2, :], inner + [top - 1, top]),
            (stacked[..., D // 2 :, :], [top] + inner + [top - 1]),
        ):
            left = [top, top - 1] + inner[::-1]
            for b in order:
                ax = left.index(b)
                left.pop(ax)
                mine = (s >> b) & 1
                keep = lax.dynamic_index_in_dim(part, mine, ax, False)
                give = lax.dynamic_index_in_dim(part, 1 - mine, ax, False)
                got = flip_shard(give, shards, b)
                part = keep.astype(f32) + got.astype(f32)
                if left:
                    part = part.astype(b16)
            sums.append(part)
        return sums

    gelu_slope, pieces_cotangent = lax.optimization_barrier((gelu_slope, pieces_cotangent))
    cotangent = assemble(own_cotangent, pieces_cotangent, groups, z, 0)
    grad_before = dot(cotangent, part_down) * gelu_slope
    grad_before_b = grad_before.astype(b16)
    hidden_two_share = dot_nt(grad_before_b, part_up)
    own_share, pieces = reduce_start(hidden_two_share, groups, z)
    sum_up = core_sum(hidden_two, grad_before_b, wide)
    block_share = dot_nt(active, part_down)
    pieces, sum_up, block_share = lax.optimization_barrier((pieces, sum_up, block_share))
    grad_hidden_two = own_share + sum(piece.astype(f32) for piece in pieces)
    own_middle = lax.dynamic_slice_in_dim(middle, z * length, length, 0)
    middle_part = jax.vjp(lambda m: layer_norm(m, gain_two, shift_two), own_middle)[1](
        grad_hidden_two
    )[0]
    grad_middle = own_upstream + middle_part
    grad_middle_b = grad_middle.astype(b16)
    grad_attended = dot_nt(grad_middle_b, full_out).astype(b16)

    columns_sent = jnp.concatenate(
        [array.reshape(length, groups, part_d) for array in (grad_attended, grad_middle_b)], axis=2
    )
    head_grad = lax.all_to_all(columns_sent.transpose(1, 0, 2), "seq", 0, 0)
    head_grad = head_grad.reshape(total, 2 * part_d)
    sum_down = core_sum(cotangent, active, wide)
    head_grad, sum_down, block_share = lax.optimization_barrier((head_grad, sum_down, block_share))
    middle_cols = head_grad[:, part_d:]

    grad_q, grad_k, grad_v = attend_back(slopes, segments[0], qkv, head_grad, part_d)
    grad_mixed = jnp.concatenate([grad_q, grad_k, grad_v], axis=1)

    mom_rows, grad_mixed = lax.optimization_barrier((mom_rows, grad_mixed))
    own_mom = lax.all_to_all(mom_rows, "seq", 0, 0).reshape(D, wide)
    halves = over_shard(
        [core_sum(hidden_one, grad_mixed, wide), core_sum(attended, middle_cols, wide), sum_up, sum_down]
    )
    own_grad_b = jnp.concatenate(halves, axis=0).astype(b16)
    held = [
        (momentum_decay * mom.astype(f32) + grad).astype(b16)
        for mom, grad in zip((own_mom[: D // 2], own_mom[D // 2 :]), halves)
    ]

    held[1], hidden_two_share, late_mixed = lax.optimization_barrier(
        (held[1], hidden_two_share, grad_mixed)
    )
    hidden_one_share = dot_nt(late_mixed, part_qkv)
    def placed(values, width):
        return lax.dynamic_update_slice_in_dim(jnp.zeros((width,), f32), values, z * values.shape[0], 0)

    share_vec = jnp.concatenate(
        [
            jnp.sum(hidden_one_share * normed_one, axis=0),
            jnp.sum(hidden_one_share, axis=0),
            placed(jnp.sum(late_mixed[:, :part_d].astype(f32), axis=0), D),
            placed(jnp.sum(late_mixed[:, 2 * part_d :].astype(f32), axis=0), D),
            jnp.sum(grad_middle, axis=0),
            jnp.sum(hidden_two_share * normed_two, axis=0),
            jnp.sum(hidden_two_share, axis=0),
            placed(jnp.sum(grad_before, axis=0), FF),
            jnp.sum(own_upstream, axis=0),
        ]
    )
    chunks = [line_seq(cut, groups) for cut in held]
    chunks, hidden_one_share, share_vec = lax.optimization_barrier(
        (chunks, hidden_one_share, share_vec)
    )
    place = z.reshape(1)
    columns_here, gram = gram_of(place, chunks, groups)
    own_grad_b, gram = lax.optimization_barrier((own_grad_b, gram))
    other = flip_shard(gram, shards, 0)
    for b in range(1, owners.bit_length() - 1):
        gram = (gram.astype(f32) + other.astype(f32)).astype(b16)
        other = flip_shard(gram, shards, b)
    grad_back = lax.all_to_all(
        own_grad_b.reshape(groups * shards, rows, wide), ("seq", "shard"), 0, 0
    )
    last = sweeps(place, gram, other, D // groups)
    own_one, one_others = reduce_start(hidden_one_share, groups, z)
    result = dot(last, columns_here).astype(b16).reshape(shards, rows, groups * wide)
    result, one_others, block_share = lax.optimization_barrier((result, one_others, block_share))
    own_block, block_others = reduce_start(block_share, groups, z)
    result = lax.all_to_all(result, "shard", 0, 0)
    result, grad_back, share_vec, block_others = lax.optimization_barrier(
        (result, grad_back, share_vec, block_others)
    )
    vec_back = lax.all_to_all(share_vec.reshape(groups * shards, 1, chunk), ("seq", "shard"), 0, 0)
    grad_hidden_one = own_one + sum(piece.astype(f32) for piece in one_others)
    block_sum = own_block + sum(piece.astype(f32) for piece in block_others)
    block_rows = (block_sum + own_middle + bias_down).astype(b16)
    own_residual = tokens_in[0].astype(f32)
    input_part = jax.vjp(lambda m: layer_norm(m, gain_one, shift_one), own_residual)[1](
        grad_hidden_one
    )[0]
    grad_rows = grad_middle + input_part

    weights = (w_qkv, w_out, w_up, w_down)
    moments = (mom_qkv, mom_out, mom_up, mom_down)
    if aligned(owners, groups):
        vmem = pl.BlockSpec(memory_space=pltpu.VMEM)
        four = tuple(jax.ShapeDtypeStruct((rows, w), f32) for w in widths)
        params = pltpu.CompilerParams(vmem_limit_bytes=24 * 2**20)
        both = pl.pallas_call(
            functools.partial(gradients_kernel, groups, owners),
            out_shape=four + four,
            in_specs=[vmem] * 5,
            out_specs=(vmem,) * 8,
            compiler_params=params,
        )(grad_back, *moments)
        grads, nexts = both[:4], both[4:]
        news = pl.pallas_call(
            functools.partial(weights_kernel, groups, owners),
            out_shape=four,
            in_specs=[pl.BlockSpec(memory_space=pltpu.SMEM)] + [vmem] * 5,
            out_specs=(vmem,) * 4,
            compiler_params=params,
        )(place, result, *weights)
    else:
        result = result.reshape(shards, rows, groups, wide)
        result = jnp.stack(
            [
                lax.dynamic_index_in_dim(result, (z - j) % groups, 2, False)
                for j in range(groups)
            ],
            axis=2,
        )
        ortho = result.reshape(4, owners, rows, groups, wide)
        grad_blocks = grad_back.reshape(groups, 4, owners, rows, wide)

        def rows_of(blocks, parts, width):
            cut = blocks[..., : width // groups // owners].reshape(rows, groups, parts, -1)
            return cut.transpose(0, 2, 1, 3).reshape(rows, width).astype(f32)

        grads, news, nexts = [], [], []
        for m in range(4):
            grad = rows_of(grad_blocks[:, m].transpose(2, 0, 1, 3), part_counts[m], widths[m])
            update = rows_of(ortho[m].transpose(1, 2, 0, 3), part_counts[m], widths[m])
            grads.append(grad)
            nexts.append(momentum_decay * moments[m] + grad)
            news.append(weights[m] - matrix_rate * 0.2 * math.sqrt(widths[m]) * update)
    grad_vec = jnp.sum(vec_back, axis=(0, 1))
    next_vec = momentum_decay * mom_vectors + grad_vec
    new_vec = vectors - vector_rate / math.sqrt(total * shards) * next_vec
    return (
        block_rows[None],
        grad_rows[None],
        *grads,
        grad_vec,
        *news,
        new_vec,
        *nexts,
        next_vec,
    )


def solution(mesh):
    tokens = P("shard", "seq", None)
    matrix = P(("seq", "shard"), None)
    vector = P(("seq", "shard"))
    five = (matrix,) * 4 + (vector,)
    return jax.shard_map(
        per_device,
        mesh=mesh,
        in_specs=(tokens, tokens, P("shard", None)) + five + five,
        out_specs=(tokens, tokens) + five + five + five,
        check_vma=False,
    )
```

```python
import functools
import math

import jax
import jax.numpy as jnp
from jax import lax
from jax.experimental import pallas as pl
from jax.experimental.pallas import tpu as pltpu
from jax.sharding import PartitionSpec as P

D = 1024
H = 16
HD = 64
FF = 4096
VEC = 12 * D

ca, cb, cc = (3.4445, -4.775, 2.0315)
momentum_decay = 0.9
matrix_rate = 0.1
vector_rate = 0.2
f32 = jnp.float32
b16 = jnp.bfloat16


def layer_norm(values, gain_vec, shift_vec):
    center = values - jnp.mean(values, axis=-1, keepdims=True)
    spread = jnp.mean(center * center, axis=-1, keepdims=True)
    return center * lax.rsqrt(spread + 1e-05) * gain_vec + shift_vec


def normed(values):
    center = values - jnp.mean(values, axis=-1, keepdims=True)
    spread = jnp.mean(center * center, axis=-1, keepdims=True)
    return center * lax.rsqrt(spread + 1e-05)


def gelu_tanh(values):
    return jax.nn.gelu(values, approximate=True)


def dot(a, b):
    return jnp.dot(a, b, preferred_element_type=f32)


def dot_nt(a, b):
    return lax.dot_general(a, b, (((1,), (1,)), ((), ())), preferred_element_type=f32)


def dot_tn(a, b):
    return lax.dot_general(a, b, (((0,), (0,)), ((), ())), preferred_element_type=f32)


def lasting(microseconds):
    return pl.CostEstimate(
        flops=microseconds * 10**7, bytes_accessed=microseconds * 10**4, transcendentals=0
    )


def spans(total):
    rows = 128
    reach = total // 2
    out = []
    for begin in range(0, total, rows):
        first = max(0, begin - reach + 1) // 128 * 128
        out.append((begin, rows, first, begin + rows - first))
    return out


def geometry(seg_q, seg_k, offset):
    shape = (seg_q.shape[0], seg_k.shape[1])
    distance = offset + lax.broadcasted_iota(jnp.int32, shape, 0) - lax.broadcasted_iota(
        jnp.int32, shape, 1
    )
    return distance.astype(f32), (distance >= 0) & (seg_q == seg_k)


def probabilities(q, k, slope, distance, allowed):
    scores = dot_nt(q * HD ** (-0.5), k) - slope * distance
    scores = jnp.where(allowed, scores, -1e30)
    terms = jnp.exp(scores - jnp.max(scores, axis=-1, keepdims=True))
    return terms * (1.0 / jnp.sum(terms, axis=-1, keepdims=True))


def attend_kernel(slopes, seg_col, seg_row, q, k, v, out):
    pair = pl.program_id(0)
    for begin, rows, first, wide in spans(q.shape[0]):
        keys = slice(first, first + wide)
        at = slice(begin, begin + rows)
        distance, allowed = geometry(seg_col[at, :], seg_row[:, keys], begin - first)
        for j in range(2):
            cols = slice(j * HD, (j + 1) * HD)
            probs = probabilities(
                q[at, cols], k[keys, cols], slopes[2 * pair + j], distance, allowed
            )
            out[at, cols] = dot(probs.astype(b16), v[keys, cols]).astype(b16)


def attend_back_kernel(slopes, seg_col, seg_row, q, k, v, g, dq, dk, dv, k_acc, v_acc):
    pair = pl.program_id(0)
    k_acc[...] = jnp.zeros_like(k_acc)
    v_acc[...] = jnp.zeros_like(v_acc)
    for begin, rows, first, wide in spans(q.shape[0]):
        keys = slice(first, first + wide)
        at = slice(begin, begin + rows)
        distance, allowed = geometry(seg_col[at, :], seg_row[:, keys], begin - first)
        for j in range(2):
            cols = slice(j * HD, (j + 1) * HD)
            q_block, g_block = q[at, cols], g[at, cols]
            probs = probabilities(q_block, k[keys, cols], slopes[2 * pair + j], distance, allowed)
            v_acc[keys, cols] += dot_tn(probs.astype(b16), g_block)
            grad_probs = dot_nt(g_block, v[keys, cols])
            inner = jnp.sum(probs * grad_probs, axis=-1, keepdims=True)
            grad_scores = (probs * (grad_probs - inner)).astype(b16)
            dq[at, cols] = (dot(grad_scores, k[keys, cols]) * HD ** (-0.5)).astype(b16)
            k_acc[keys, cols] += dot_tn(grad_scores, q_block)
    dk[...] = (k_acc[...] * HD ** (-0.5)).astype(b16)
    dv[...] = v_acc[...].astype(b16)


def attention_specs(total, pairs):
    col = pl.BlockSpec((total, 1), lambda p: (0, 0))
    row = pl.BlockSpec((1, total), lambda p: (0, 0))
    parts = [
        pl.BlockSpec((total, 2 * HD), lambda p, base=base: (0, base * pairs + p))
        for base in range(3)
    ]
    return [pl.BlockSpec(memory_space=pltpu.SMEM), col, row] + parts


def attend(slopes, seg, qkv, wide):
    total = qkv.shape[0]
    pairs = wide // (2 * HD)
    return pl.pallas_call(
        attend_kernel,
        grid=(pairs,),
        out_shape=jax.ShapeDtypeStruct((total, wide), b16),
        in_specs=attention_specs(total, pairs),
        out_specs=pl.BlockSpec((total, 2 * HD), lambda p: (0, p)),
        compiler_params=pltpu.CompilerParams(vmem_limit_bytes=24 * 2**20),
        cost_estimate=lasting(7),
    )(slopes, seg.reshape(total, 1), seg.reshape(1, total), qkv, qkv, qkv)


def attend_back(slopes, seg, qkv, grad, wide):
    total = qkv.shape[0]
    pairs = wide // (2 * HD)
    pair_spec = pl.BlockSpec((total, 2 * HD), lambda p: (0, p))
    part = jax.ShapeDtypeStruct((total, wide), b16)
    return pl.pallas_call(
        attend_back_kernel,
        grid=(pairs,),
        out_shape=(part, part, part),
        in_specs=attention_specs(total, pairs) + [pair_spec],
        out_specs=(pair_spec, pair_spec, pair_spec),
        scratch_shapes=[pltpu.VMEM((total, 2 * HD), f32), pltpu.VMEM((total, 2 * HD), f32)],
        compiler_params=pltpu.CompilerParams(vmem_limit_bytes=24 * 2**20),
        cost_estimate=lasting(11),
    )(slopes, seg.reshape(total, 1), seg.reshape(1, total), qkv, qkv, qkv, grad)


def gram_kernel(groups, place, *refs):
    blocks, (columns, gram) = refs[:-2], refs[-2:]
    each = 2 * groups - 1
    tall, wide = blocks[0].shape
    for part in range(len(blocks) // each):
        own, right, left = (
            blocks[part * each],
            blocks[part * each + 1 : part * each + groups],
            blocks[part * each + groups : (part + 1) * each],
        )
        at = slice(part * tall, (part + 1) * tall)
        columns[at, :wide] = own[...]
        for k in range(1, groups):
            cols = slice(k * wide, (k + 1) * wide)

            @pl.when(place[0] >= k)
            def _(source=right[k - 1], at=at, cols=cols):
                columns[at, cols] = source[...]

            @pl.when(place[0] < k)
            def _(source=left[groups - k - 1], at=at, cols=cols):
                columns[at, cols] = source[...]

    step = 256

    def one(i, carry):
        cut = pl.ds(i * step, step)
        gram[cut, :] = dot_nt(columns[cut, :], columns[...]).astype(b16)
        return carry

    lax.fori_loop(0, D // step, one, 0)


def gram_of(place, chunks, groups):
    blocks = [block for chunk in chunks for block in chunk]
    vmem = pl.BlockSpec(memory_space=pltpu.VMEM)
    wide = blocks[0].shape[1] * groups
    return pl.pallas_call(
        functools.partial(gram_kernel, groups),
        out_shape=(jax.ShapeDtypeStruct((D, wide), b16), jax.ShapeDtypeStruct((D, D), b16)),
        in_specs=[pl.BlockSpec(memory_space=pltpu.SMEM)] + [vmem] * len(blocks),
        out_specs=(vmem, vmem),
        compiler_params=pltpu.CompilerParams(vmem_limit_bytes=40 * 2**20),
        cost_estimate=lasting(8),
    )(place, *blocks)


def sweeps_kernel(place, mine, other, out, a_zero, a_zero_b, r_zero, a_one, a_one_b, r_one):
    step = 256
    span = out.shape[0]

    def blocks(body):
        def one(i, carry):
            body(pl.ds(i * step, step))
            return carry

        lax.fori_loop(0, D // step, one, 0)

    trace = jnp.zeros((1, 1), f32)
    for i in range(D // step):
        cut = slice(i * step, (i + 1) * step)
        gram = mine[cut, :].astype(f32) + other[cut, :].astype(f32)
        a_zero[cut, :] = gram
        at = lax.broadcasted_iota(jnp.int32, (step, D), 0) + i * step
        kept = jnp.where(at == lax.broadcasted_iota(jnp.int32, (step, D), 1), gram, 0.0)
        trace = trace + jnp.sum(jnp.sum(kept, axis=1, keepdims=True), axis=0, keepdims=True)
    factor = 1.0 / (jnp.sqrt(trace) + 1e-07)
    square_factor = factor * factor

    def scale(cut):
        scaled = a_zero[cut, :] * square_factor
        a_zero[cut, :] = scaled
        a_zero_b[cut, :] = scaled.astype(b16)

    def first(cut):
        r_zero[cut, :] = (cb * a_zero[cut, :] + cc * dot(a_zero_b[cut, :], a_zero_b[...])).astype(b16)

    def second(cut):
        once = ca * a_zero[cut, :] + dot(a_zero_b[cut, :], r_zero[...])
        twice = ca * once + dot(once.astype(b16), r_zero[...])
        a_one[cut, :] = twice
        a_one_b[cut, :] = twice.astype(b16)

    def third(cut):
        r_one[cut, :] = (cb * a_one[cut, :] + cc * dot(a_one_b[cut, :], a_one_b[...])).astype(b16)

    for body in (scale, first, second, third):
        blocks(body)
    begin = place[0] * span

    def by_p_one(values):
        return ca * values + dot(values.astype(b16), r_one[...])

    lead = by_p_one(by_p_one(a_one[pl.ds(begin, span), :]))
    square = by_p_one(by_p_one(dot(lead.astype(b16), a_one_b[...])))
    at = lax.broadcasted_iota(jnp.int32, (span, D), 0) + begin
    unit = jnp.where(at == lax.broadcasted_iota(jnp.int32, (span, D), 1), ca, 0.0)
    last = by_p_one(unit + cb * lead + cc * square)
    last = ca * last + dot(last.astype(b16), r_zero[...])
    out[...] = (last * factor).astype(b16)


def sweeps(place, mine, other, span):
    whole = pl.BlockSpec(memory_space=pltpu.VMEM)
    return pl.pallas_call(
        sweeps_kernel,
        out_shape=jax.ShapeDtypeStruct((span, D), b16),
        in_specs=[pl.BlockSpec(memory_space=pltpu.SMEM), whole, whole],
        out_specs=whole,
        scratch_shapes=[
            pltpu.VMEM((D, D), f32),
            pltpu.VMEM((D, D), b16),
            pltpu.VMEM((D, D), b16),
            pltpu.VMEM((D, D), f32),
            pltpu.VMEM((D, D), b16),
            pltpu.VMEM((D, D), b16),
        ],
        compiler_params=pltpu.CompilerParams(vmem_limit_bytes=40 * 2**20),
        cost_estimate=lasting(18),
    )(place, mine, other)


widths = (3 * D, D, FF, FF)
part_counts = (3, 1, 1, 1)


def column_runs(m, owners, groups, c):
    run = widths[m] // part_counts[m] // groups
    size = widths[m] // groups // owners
    out = []
    at = c * size
    while at < (c + 1) * size:
        part, inner = at // run, at % run
        count = min(run - inner, (c + 1) * size - at)
        out.append((at - c * size, part * (widths[m] // part_counts[m]) + inner, run, count))
        at += count
    return out


def aligned(owners, groups):
    return all(
        number % 128 == 0
        for m in range(4)
        for c in range(owners)
        for runs in column_runs(m, owners, groups, c)
        for number in runs
    )


def gradients_kernel(groups, owners, blocks, *refs):
    moments, grads, nexts = refs[:4], refs[4:8], refs[8:]
    for m in range(4):
        for c in range(owners):
            for z in range(groups):
                for inside, first, apart, count in column_runs(m, owners, groups, c):
                    cols = slice(first + z * apart, first + z * apart + count)
                    source = blocks[(z * 4 + m) * owners + c, :, inside : inside + count]
                    grad = source.astype(f32)
                    grads[m][:, cols] = grad
                    nexts[m][:, cols] = momentum_decay * moments[m][:, cols] + grad


def weights_kernel(groups, owners, place, blocks, *refs):
    weights, news = refs[:4], refs[4:]
    wide = blocks.shape[2] // groups
    for m in range(4):
        rate = matrix_rate * 0.2 * math.sqrt(widths[m])
        for c in range(owners):
            for k in range(groups):
                z = lax.rem(place[0] - k + groups, groups)
                for inside, first, apart, count in column_runs(m, owners, groups, c):
                    cols = pl.ds(pl.multiple_of(first + z * apart, 128), count)
                    begin = k * wide + inside
                    update = blocks[m * owners + c, :, begin : begin + count].astype(f32)
                    news[m][:, cols] = weights[m][:, cols] - rate * update


def shift_seq(array, groups, k):
    return lax.ppermute(array, "seq", [(i, (i + k) % groups) for i in range(groups)])


def flip_shard(array, shards, bit):
    return lax.ppermute(array, "shard", [(i, i ^ (1 << bit)) for i in range(shards)])


def rotations(array, groups):
    return [shift_seq(array, groups, k) for k in range(1, groups)]


def assemble(own, pieces, groups, z, axis):
    size = own.shape[axis]
    shape = list(own.shape)
    shape[axis] = size * groups
    full = jnp.zeros(shape, own.dtype)
    for k, piece in enumerate([own] + pieces):
        full = lax.dynamic_update_slice_in_dim(full, piece, (z - k) % groups * size, axis)
    return full


def gather_seq(array, groups, z, axis):
    return assemble(array, rotations(array, groups), groups, z, axis)


def exchange(blocks, groups, z):
    own = lax.dynamic_index_in_dim(blocks, z, 0, True)
    pieces = [
        shift_seq(lax.dynamic_index_in_dim(blocks, (z + k) % groups, 0, True), groups, k)
        for k in range(1, groups)
    ]
    return own, pieces


def reduce_start(array, groups, z):
    size = array.shape[0] // groups
    own = lax.dynamic_slice_in_dim(array, z * size, size, 0)
    pieces = []
    for k in range(1, groups):
        block = lax.dynamic_slice_in_dim(array, (z + k) % groups * size, size, 0)
        pieces.append(shift_seq(block.astype(b16), groups, k))
    return own, pieces


def line_seq(array, groups):
    right, left = [], []
    from_left = from_right = array
    for _ in range(groups - 1):
        from_left = lax.ppermute(from_left, "seq", [(i, i + 1) for i in range(groups - 1)])
        from_right = lax.ppermute(from_right, "seq", [(i + 1, i) for i in range(groups - 1)])
        right.append(from_left)
        left.append(from_right)
    return [array] + right + left


def per_device(
    tokens_in,
    out_grad,
    segments,
    w_qkv,
    w_out,
    w_up,
    w_down,
    vectors,
    mom_qkv,
    mom_out,
    mom_up,
    mom_down,
    mom_vectors,
):
    groups = lax.axis_size("seq")
    shards = lax.axis_size("shard")
    z = lax.axis_index("seq")
    s = lax.axis_index("shard")
    length = tokens_in.shape[1]
    total = length * groups
    rows = w_qkv.shape[0]
    owners = shards // 4
    part_d = D // groups
    part_f = FF // groups
    wide = part_f // owners
    chunk = vectors.shape[0]

    def columns_of(matrix, parts):
        split = matrix.astype(b16).reshape(rows, parts, groups, -1)
        return split.transpose(2, 0, 1, 3).reshape(groups, rows, -1)

    lanes = min(chunk, 128)
    vec_rows = chunk // lanes
    vec_block = jnp.pad(
        vectors.astype(b16).reshape(vec_rows, lanes), ((0, rows - vec_rows), (0, 128 - lanes))
    )
    send_a = jnp.concatenate(
        [columns_of(w_qkv, 3), jnp.broadcast_to(vec_block, (groups, rows, 128))], axis=2
    )
    got_a = assemble(*exchange(send_a, groups, z), groups, z, 0)
    all_a = lax.all_gather(got_a, "shard", axis=1).reshape(groups * shards, rows, -1)
    wide_qkv = all_a.reshape(D, -1)
    part_qkv = wide_qkv[:, : 3 * part_d]
    full_vec = all_a[:, :vec_rows, 3 * part_d : 3 * part_d + lanes].reshape(VEC).astype(f32).reshape(12, D)
    send_b = jnp.concatenate(
        [
            jnp.broadcast_to(w_out.astype(b16), (groups, rows, D)),
            columns_of(w_up, 1),
            columns_of(w_down, 1),
        ],
        axis=2,
    )
    send_b, _ = lax.optimization_barrier((send_b, got_a))
    got_b = lax.all_to_all(send_b, "seq", 0, 0)
    own_tokens, got_b = lax.optimization_barrier((tokens_in[0], got_b))
    all_b = lax.all_gather(got_b, "shard", axis=1).reshape(D, -1)
    full_out = all_b[:, :D]
    part_up = all_b[:, D : D + part_f]
    part_down = all_b[:, D + part_f :]
    pieces_tokens = rotations(own_tokens, groups)
    def blocks_of(matrix, parts):
        split = matrix.astype(b16).reshape(rows, parts, groups, -1).transpose(0, 2, 1, 3)
        split = split.reshape(rows, groups, owners, -1)
        return jnp.pad(split, ((0, 0), (0, 0), (0, 0), (0, wide - split.shape[3])))

    mom_blocks = jnp.stack(
        [
            blocks_of(moment, parts)
            for moment, parts in zip((mom_qkv, mom_out, mom_up, mom_down), part_counts)
        ]
    )
    mom_blocks = mom_blocks.transpose(0, 3, 2, 1, 4).reshape(shards, groups, rows, wide)
    mom_blocks, _ = lax.optimization_barrier((mom_blocks, got_b))
    mom_rows = lax.all_to_all(mom_blocks, "shard", 0, 0)
    mom_rows = mom_rows.transpose(1, 0, 2, 3).reshape(groups, shards * rows, wide)
    pieces_tokens, own_cotangent = lax.optimization_barrier((pieces_tokens, out_grad[0]))
    pieces_cotangent = rotations(own_cotangent, groups)
    tokens_all = assemble(own_tokens, pieces_tokens, groups, z, 0)
    residual = tokens_all.astype(f32)

    gain_one, shift_one, bias_query, bias_value, bias_out, gain_two, shift_two = (
        full_vec[i] for i in range(7)
    )
    bias_up = lax.dynamic_slice_in_dim(full_vec[7:11].reshape(FF), z * part_f, part_f, 0)
    bias_down = full_vec[11]
    part_bias = jnp.concatenate(
        [
            lax.dynamic_slice_in_dim(bias_query, z * part_d, part_d, 0),
            jnp.zeros((part_d,), f32),
            lax.dynamic_slice_in_dim(bias_value, z * part_d, part_d, 0),
            jnp.zeros((128,), f32),
        ]
    )

    normed_one = normed(residual)
    hidden_one = (normed_one * gain_one + shift_one).astype(b16)
    qkv = (dot(hidden_one, wide_qkv) + part_bias).astype(b16)
    head_count = part_d // HD
    heads = (z * head_count + jnp.arange(head_count)).astype(f32)
    slopes = jnp.exp2(-8.0 * (heads + 1.0) / H)
    attended_part = attend(slopes, segments[0], qkv, part_d)
    pieces_cotangent, attended_part = lax.optimization_barrier((pieces_cotangent, attended_part))
    pieces_attended = rotations(attended_part, groups)
    attended = assemble(attended_part, pieces_attended, groups, z, 1)

    middle = residual + dot(attended, full_out) + bias_out
    normed_two = normed(middle)
    hidden_two = (normed_two * gain_two + shift_two).astype(b16)
    before = dot(hidden_two, part_up) + bias_up
    active_wide, gelu_back = jax.vjp(gelu_tanh, before)
    active = active_wide.astype(b16)
    gelu_slope = gelu_back(jnp.ones_like(before))[0]
    own_upstream = out_grad[0].astype(f32)

    low = s & 1

    def core_sum(left, right, padded):
        size = right.shape[1] // owners

        def half(bit):
            cuts = [
                lax.dynamic_slice_in_dim(right, (2 * high + bit) * size, size, 1)
                for high in range(owners // 2)
            ]
            return jnp.stack([dot_tn(left, cut).astype(b16) for cut in cuts])

        got = flip_shard(half(1 - low), shards, 0)
        both = (half(low).astype(f32) + got.astype(f32)).astype(b16)
        return jnp.pad(both, ((0, 0), (0, 0), (0, padded - size)))

    top = shards.bit_length() - 2
    inner = list(range(1, top - 1))

    def over_shard(four):
        stacked = jnp.stack(four)
        stacked = stacked.reshape([2] * (2 + len(inner)) + list(stacked.shape[2:]))
        sums = []
        for part, order in (
            (stacked[..., : D // 2, :], inner + [top - 1, top]),
            (stacked[..., D // 2 :, :], [top] + inner + [top - 1]),
        ):
            left = [top, top - 1] + inner[::-1]
            for b in order:
                ax = left.index(b)
                left.pop(ax)
                mine = (s >> b) & 1
                keep = lax.dynamic_index_in_dim(part, mine, ax, False)
                give = lax.dynamic_index_in_dim(part, 1 - mine, ax, False)
                got = flip_shard(give, shards, b)
                part = keep.astype(f32) + got.astype(f32)
                if left:
                    part = part.astype(b16)
            sums.append(part)
        return sums

    gelu_slope, pieces_cotangent = lax.optimization_barrier((gelu_slope, pieces_cotangent))
    cotangent = assemble(own_cotangent, pieces_cotangent, groups, z, 0)
    grad_before = dot(cotangent, part_down) * gelu_slope
    grad_before_b = grad_before.astype(b16)
    hidden_two_share = dot_nt(grad_before_b, part_up)
    own_share, pieces = reduce_start(hidden_two_share, groups, z)
    sum_up = core_sum(hidden_two, grad_before_b, wide)
    block_share = dot_nt(active, part_down)
    pieces, sum_up, block_share = lax.optimization_barrier((pieces, sum_up, block_share))
    grad_hidden_two = own_share + sum(piece.astype(f32) for piece in pieces)
    own_middle = lax.dynamic_slice_in_dim(middle, z * length, length, 0)
    middle_part = jax.vjp(lambda m: layer_norm(m, gain_two, shift_two), own_middle)[1](
        grad_hidden_two
    )[0]
    grad_middle = own_upstream + middle_part
    grad_middle_b = grad_middle.astype(b16)
    grad_attended = dot_nt(grad_middle_b, full_out).astype(b16)

    columns_sent = jnp.concatenate(
        [array.reshape(length, groups, part_d) for array in (grad_attended, grad_middle_b)], axis=2
    )
    head_grad = lax.all_to_all(columns_sent.transpose(1, 0, 2), "seq", 0, 0)
    head_grad = head_grad.reshape(total, 2 * part_d)
    sum_down = core_sum(cotangent, active, wide)
    head_grad, sum_down, block_share = lax.optimization_barrier((head_grad, sum_down, block_share))
    middle_cols = head_grad[:, part_d:]

    grad_q, grad_k, grad_v = attend_back(slopes, segments[0], qkv, head_grad, part_d)
    grad_mixed = jnp.concatenate([grad_q, grad_k, grad_v], axis=1)

    mom_rows, grad_mixed = lax.optimization_barrier((mom_rows, grad_mixed))
    own_mom = lax.all_to_all(mom_rows, "seq", 0, 0).reshape(D, wide)
    halves = over_shard(
        [core_sum(hidden_one, grad_mixed, wide), core_sum(attended, middle_cols, wide), sum_up, sum_down]
    )
    own_grad_b = jnp.concatenate(halves, axis=0).astype(b16)
    held = [
        (momentum_decay * mom.astype(f32) + grad).astype(b16)
        for mom, grad in zip((own_mom[: D // 2], own_mom[D // 2 :]), halves)
    ]

    held[1], hidden_two_share, late_mixed = lax.optimization_barrier(
        (held[1], hidden_two_share, grad_mixed)
    )
    hidden_one_share = dot_nt(late_mixed, part_qkv)
    def placed(values, width):
        return lax.dynamic_update_slice_in_dim(jnp.zeros((width,), f32), values, z * values.shape[0], 0)

    share_vec = jnp.concatenate(
        [
            jnp.sum(hidden_one_share * normed_one, axis=0),
            jnp.sum(hidden_one_share, axis=0),
            placed(jnp.sum(late_mixed[:, :part_d].astype(f32), axis=0), D),
            placed(jnp.sum(late_mixed[:, 2 * part_d :].astype(f32), axis=0), D),
            jnp.sum(grad_middle, axis=0),
            jnp.sum(hidden_two_share * normed_two, axis=0),
            jnp.sum(hidden_two_share, axis=0),
            placed(jnp.sum(grad_before, axis=0), FF),
            jnp.sum(own_upstream, axis=0),
        ]
    )
    chunks = [line_seq(cut, groups) for cut in held]
    chunks, hidden_one_share, share_vec = lax.optimization_barrier(
        (chunks, hidden_one_share, share_vec)
    )
    place = z.reshape(1)
    columns_here, gram = gram_of(place, chunks, groups)
    own_grad_b, gram = lax.optimization_barrier((own_grad_b, gram))
    other = flip_shard(gram, shards, 0)
    for b in range(1, owners.bit_length() - 1):
        gram = (gram.astype(f32) + other.astype(f32)).astype(b16)
        other = flip_shard(gram, shards, b)
    grad_back = lax.all_to_all(
        own_grad_b.reshape(groups * shards, rows, wide), ("seq", "shard"), 0, 0
    )
    last = sweeps(place, gram, other, D // groups)
    own_one, one_others = reduce_start(hidden_one_share, groups, z)
    result = dot(last, columns_here).astype(b16).reshape(shards, rows, groups * wide)
    result, one_others, block_share = lax.optimization_barrier((result, one_others, block_share))
    own_block, block_others = reduce_start(block_share, groups, z)
    result = lax.all_to_all(result, "shard", 0, 0)
    result, grad_back, share_vec, block_others = lax.optimization_barrier(
        (result, grad_back, share_vec, block_others)
    )
    vec_back = lax.all_to_all(share_vec.reshape(groups * shards, 1, chunk), ("seq", "shard"), 0, 0)
    grad_hidden_one = own_one + sum(piece.astype(f32) for piece in one_others)
    block_sum = own_block + sum(piece.astype(f32) for piece in block_others)
    block_rows = (block_sum + own_middle + bias_down).astype(b16)
    own_residual = tokens_in[0].astype(f32)
    input_part = jax.vjp(lambda m: layer_norm(m, gain_one, shift_one), own_residual)[1](
        grad_hidden_one
    )[0]
    grad_rows = grad_middle + input_part

    weights = (w_qkv, w_out, w_up, w_down)
    moments = (mom_qkv, mom_out, mom_up, mom_down)
    if aligned(owners, groups):
        vmem = pl.BlockSpec(memory_space=pltpu.VMEM)
        four = tuple(jax.ShapeDtypeStruct((rows, w), f32) for w in widths)
        params = pltpu.CompilerParams(vmem_limit_bytes=24 * 2**20)
        both = pl.pallas_call(
            functools.partial(gradients_kernel, groups, owners),
            out_shape=four + four,
            in_specs=[vmem] * 5,
            out_specs=(vmem,) * 8,
            compiler_params=params,
        )(grad_back, *moments)
        grads, nexts = both[:4], both[4:]
        news = pl.pallas_call(
            functools.partial(weights_kernel, groups, owners),
            out_shape=four,
            in_specs=[pl.BlockSpec(memory_space=pltpu.SMEM)] + [vmem] * 5,
            out_specs=(vmem,) * 4,
            compiler_params=params,
        )(place, result, *weights)
    else:
        result = result.reshape(shards, rows, groups, wide)
        result = jnp.stack(
            [
                lax.dynamic_index_in_dim(result, (z - j) % groups, 2, False)
                for j in range(groups)
            ],
            axis=2,
        )
        ortho = result.reshape(4, owners, rows, groups, wide)
        grad_blocks = grad_back.reshape(groups, 4, owners, rows, wide)

        def rows_of(blocks, parts, width):
            cut = blocks[..., : width // groups // owners].reshape(rows, groups, parts, -1)
            return cut.transpose(0, 2, 1, 3).reshape(rows, width).astype(f32)

        grads, news, nexts = [], [], []
        for m in range(4):
            grad = rows_of(grad_blocks[:, m].transpose(2, 0, 1, 3), part_counts[m], widths[m])
            update = rows_of(ortho[m].transpose(1, 2, 0, 3), part_counts[m], widths[m])
            grads.append(grad)
            nexts.append(momentum_decay * moments[m] + grad)
            news.append(weights[m] - matrix_rate * 0.2 * math.sqrt(widths[m]) * update)
    grad_vec = jnp.sum(vec_back, axis=(0, 1))
    next_vec = momentum_decay * mom_vectors + grad_vec
    new_vec = vectors - vector_rate / math.sqrt(total * shards) * next_vec
    return (
        block_rows[None],
        grad_rows[None],
        *grads,
        grad_vec,
        *news,
        new_vec,
        *nexts,
        next_vec,
    )


def solution(mesh):
    tokens = P("shard", "seq", None)
    matrix = P(("seq", "shard"), None)
    vector = P(("seq", "shard"))
    five = (matrix,) * 4 + (vector,)
    return jax.shard_map(
        per_device,
        mesh=mesh,
        in_specs=(tokens, tokens, P("shard", None)) + five + five,
        out_specs=(tokens, tokens) + five + five + five,
        check_vma=False,
    )
```
